32 devices in a mesh: shift: 4 (over y, x), space: 8 (over z, core).
Axes of the slice: x: 2, y: 2, z: 4, core: 2. Of those that a mesh axis runs over, the one named last changes fastest.
Arguments:
- residual: float32 [4, 128, 128, 128], P('shift', 'space'), may hold values from -6 to 6
- log_base: bfloat16 [128, 128, 128], P('space'), may hold values from -3 to 3
- mask: int32 [16, 16, 16], replicated, may hold values from 0 to 1
- gen_vector: int32 [64], replicated, may hold values from 1 to 1023
- point_index: int32 [4], P('shift'), may hold values from 0 to 1023
- shift_values: float32 [4, 64], P('shift'), may hold values from 0 to 1
Outputs:
- correction: float32 [4, 128, 128, 128], P('shift', 'space')
- mean_field: float32 [128, 128, 128], P('space', 'shift')
- square_field: float32 [128, 128, 128], P('space', 'shift')
The draws below stay inside these ranges and needn't reach their ends.
All inputs are finite; a program needn't handle non-finite values.
Results may differ from the reference program's by a relative error of at most 0.0003.
Values sent between devices are 32-bit elements; how exact they have to be, the bound alone decides.
A program may use at most 192 MiB of HBM per device.

```python
import math
import jax
import jax.numpy as jnp
from jax import lax

YZ = 128
MODES = 64
NPTS = 1024
SWEEPS_LOW = 8
SHIFTS = 4
NX = 128


def draw_mask(key, part):
    rows = NX // 8
    cols = YZ // 8
    level = jax.random.randint(key, (rows, cols, cols), 0, 8)
    limit = 2 + 6 * jnp.arange(rows, dtype=jnp.int32) // max(rows - 1, 1)
    return (level < limit[:, None, None]).astype(jnp.int32)


def set_ends(values, key, least, top_value):
    longest = values.shape.index(max(values.shape))
    spots = []
    for shift in (0, 1):
        where = [jax.random.randint(jax.random.fold_in(key, axis), (), 0, length) for axis, length in enumerate(values.shape)]
        where[longest] = (where[longest] + shift) % values.shape[longest]
        spots.append(tuple(where))
    return values.at[spots[0]].set(least).at[spots[1]].set(top_value)


def with_spikes(drawn, own_key, source, target, parts, factor):
    def block_of(dim):
        return (jnp.arange(drawn.shape[dim]) // (drawn.shape[dim] // parts)).reshape((-1,) + (1,) * (drawn.ndim - 1 - dim))

    one_side = jax.random.permutation(own_key, parts)[block_of(target)]
    second = (block_of(target) + parts // 2) % parts
    return jnp.where((block_of(source) == one_side) | (block_of(source) == second), factor * drawn, drawn)


def block_scale(stream_key, shape, split, least, largest):
    def one(dim, shards_of):
        steps = jax.random.uniform(jax.random.fold_in(jax.random.fold_in(stream_key, 6), dim), (shards_of,), jnp.float32, least / len(split), largest / len(split))
        return jnp.repeat(jnp.exp(steps), shape[dim] // shards_of).reshape((-1,) + (1,) * (len(shape) - dim - 1))

    loudness = one(*split[0])
    for cut in split[1:]:
        loudness = loudness * one(*cut)
    return loudness


def normal_values(rng, shape, width, most, cuts=(), held_as=jnp.bfloat16):
    array = jax.random.normal(rng, shape, jnp.float32) * width
    if len(cuts) > 0:
        array = block_scale(rng, shape, cuts, -0.22, 0.18) * array
    return jnp.clip(array, min=-most, max=most).astype(held_as)


def noise_with(rng, shape, scale, bound, pieces, heavy, held_as=jnp.bfloat16):
    entries = scale * jax.random.normal(rng, shape, jnp.float32)
    if pieces:
        entries = entries * block_scale(rng, shape, pieces, -0.22, 0.18)
    return jnp.clip(with_spikes(entries, jax.random.fold_in(rng, 3), *heavy), -bound, bound).astype(held_as)


def setup_inputs(seed: int = 0) -> dict:
    key_list = jax.random.split(jax.random.key(seed), 7)
    return {
        "residual": noise_with(key_list[0], (SHIFTS, NX, YZ, YZ), 1.0, 6.0, ((0, 4), (1, 8)), (0, 2, 4, 2.0), jnp.float32),
        "log_base": normal_values(key_list[1], (NX, YZ, YZ), 0.5, 3.0, ((0, 8),)),
        "mask": draw_mask(jax.random.fold_in(key_list[6], 71), 0),
        "gen_vector": set_ends(jax.random.randint(key_list[3], (MODES,), 1, NPTS), jax.random.fold_in(key_list[3], 1), 1, NPTS - 1).astype(jnp.int32),
        "point_index": set_ends(jax.random.randint(key_list[4], (SHIFTS,), 0, NPTS), jax.random.fold_in(key_list[4], 1), 0, NPTS - 1).astype(jnp.int32),
        "shift_values": jnp.clip(1.0 * jax.random.uniform(key_list[5], (SHIFTS, MODES), jnp.float32) ** block_scale(key_list[5], (SHIFTS, MODES), ((0, 4),), -0.2, 0.2), 0.0, 1.0),
    }


RELAX = 0.8

def mode_tables(modes):
    order = jnp.arange(modes, dtype=jnp.int32)
    along_x = (order % 4 + 1).astype(jnp.float32)
    along_y = (order // 4 % 4 + 1).astype(jnp.float32)
    along_z = (order // 16 + 1).astype(jnp.float32)
    amplitude = 1.5 / jnp.sqrt(along_x * along_x + along_y * along_y + along_z * along_z)
    return (along_x, along_y, along_z, amplitude)

def cosine_table(frequency, cells, start, total):
    position = (jnp.arange(cells, dtype=jnp.int32) + start).astype(jnp.float32) + 0.5
    return jnp.cos(math.pi * frequency[:, None] * position[None, :] / total)

def lattice_sample(point, generator, offset):
    lattice = point * generator % NPTS
    shifted = lattice.astype(jnp.float32) / NPTS + offset
    fraction = shifted - jnp.floor(shifted)
    return 1.0 - 2.0 * jnp.abs(2.0 * fraction - 1.0)

def smooth_log(sample, table_x, table_y, table_z, amplitude):
    weights = (amplitude * sample)[:, None] * table_x
    outer = weights[:, :, None] * table_y[:, None, :]
    modes, rows, cols = outer.shape
    flat = outer.reshape(modes, rows * cols)
    product = lax.dot_general(flat, table_z, (((0,), (0,)), ((), ())), precision=lax.Precision.HIGHEST, preferred_element_type=jnp.float32)
    return product.reshape(rows, cols, table_z.shape[1])

def face_weights(conduct_wide):
    center = conduct_wide[1:-1]
    padded = jnp.pad(center, ((0, 0), (1, 1), (1, 1)), mode='edge')
    face_west = 0.5 * (center + conduct_wide[:-2])
    face_east = 0.5 * (center + conduct_wide[2:])
    face_south = 0.5 * (center + padded[:, :-2, 1:-1])
    face_north = 0.5 * (center + padded[:, 2:, 1:-1])
    face_below = 0.5 * (center + padded[:, 1:-1, :-2])
    face_above = 0.5 * (center + padded[:, 1:-1, 2:])
    diagonal = face_west + face_east + face_south + face_north + face_below + face_above
    return (face_west, face_east, face_south, face_north, face_below, face_above, diagonal)

def apply_level(conduct_wide, field_wide):
    face_west, face_east, face_south, face_north, face_below, face_above, diagonal = face_weights(conduct_wide)
    inner = field_wide[1:-1]
    zeroed = jnp.pad(inner, ((0, 0), (1, 1), (1, 1)))
    beside = face_west * field_wide[:-2] + face_east * field_wide[2:]
    beside = beside + face_south * zeroed[:, :-2, 1:-1] + face_north * zeroed[:, 2:, 1:-1]
    beside = beside + face_below * zeroed[:, 1:-1, :-2] + face_above * zeroed[:, 1:-1, 2:]
    return (diagonal, diagonal * inner - beside)

def expand_blocks(blocks, size):
    rows, cols, depth = blocks.shape
    grown = jnp.broadcast_to(blocks[:, None, :, None, :, None], (rows, size, cols, size, depth, size))
    return grown.reshape(rows * size, cols * size, depth * size)

def coarsen(values):
    rows, cols, depth = values.shape
    return values.reshape(rows // 2, 2, cols // 2, 2, depth // 2, 2).sum(axis=(1, 3, 5))

def refine(values):
    rows, cols, depth = values.shape
    grown = jnp.broadcast_to(values[:, None, :, None, :, None], (rows, 2, cols, 2, depth, 2))
    return grown.reshape(rows * 2, cols * 2, depth * 2)

def widen_conduct(conduct):
    return jnp.pad(conduct, ((1, 1), (0, 0), (0, 0)), mode='edge')

def widen_field(field):
    return jnp.pad(field, ((1, 1), (0, 0), (0, 0)))

def relax(solution, source, conduct_wide, active, sweeps):
    for repeat in range(sweeps):
        diagonal, applied = apply_level(conduct_wide, widen_field(solution))
        solution = active * (solution + RELAX * (source - applied) / diagonal)
    return solution

def defect(solution, source, conduct_wide, active):
    diagonal, applied = apply_level(conduct_wide, widen_field(solution))
    return active * (source - applied)

def reference(residual, log_base, mask, gen_vector, point_index, shift_values):
    along_x, along_y, along_z, amplitude = mode_tables(MODES)
    table_x = cosine_table(along_x, NX, 0, NX)
    table_y = cosine_table(along_y, YZ, 0, YZ)
    table_z = cosine_table(along_z, YZ, 0, YZ)
    blocks = mask.astype(jnp.float32)
    active_top = expand_blocks(blocks, 8)
    active_mid = expand_blocks(blocks, 4)
    active_low = expand_blocks(blocks, 2)
    base = log_base.astype(jnp.float32)

    def one_shift(inputs):
        source_top, point, offset = inputs
        sample = lattice_sample(point, gen_vector, offset)
        conduct_top = jnp.exp(base + smooth_log(sample, table_x, table_y, table_z, amplitude))
        conduct_mid = 0.125 * coarsen(conduct_top)
        conduct_low = 0.125 * coarsen(conduct_mid)
        wide_top = widen_conduct(conduct_top)
        wide_mid = widen_conduct(conduct_mid)
        wide_low = widen_conduct(conduct_low)
        solution_top = relax(jnp.zeros_like(source_top), source_top, wide_top, active_top, 2)
        source_mid = 0.5 * coarsen(defect(solution_top, source_top, wide_top, active_top))
        solution_mid = relax(jnp.zeros_like(source_mid), source_mid, wide_mid, active_mid, 2)
        source_low = 0.5 * coarsen(defect(solution_mid, source_mid, wide_mid, active_mid))
        solution_low = relax(jnp.zeros_like(source_low), source_low, wide_low, active_low, SWEEPS_LOW)
        solution_mid = relax(solution_mid + refine(solution_low), source_mid, wide_mid, active_mid, 2)
        return relax(solution_top + refine(solution_mid), source_top, wide_top, active_top, 2)
    correction = lax.map(one_shift, (residual, point_index, shift_values))
    mean_field = lax.optimization_barrier(jnp.sum(correction, axis=0)) / SHIFTS
    square_field = lax.optimization_barrier(jnp.sum(correction * correction, axis=0)) / SHIFTS
    return (correction, mean_field, square_field)
```

```python
import functools
import math

import jax
import jax.numpy as jnp
import numpy as np
from jax import lax
from jax.experimental import pallas as pl
from jax.experimental.pallas import tpu as pltpu
from jax.sharding import PartitionSpec as P

NPTS = 1024
SWEEPS_LOW = 8
RELAX = 0.8
MESH = pl.DeviceIdType.MESH
HIGHEST = lax.Precision.HIGHEST
GROUPS = 4


def exact_dot(a, b):
    return jnp.dot(a, b, precision=HIGHEST, preferred_element_type=jnp.float32)


def flag_dot(a, b):
    return jnp.dot(
        a.astype(jnp.bfloat16), b.astype(jnp.bfloat16), preferred_element_type=jnp.float32
    )


def iota(shape, dim):
    return lax.broadcasted_iota(jnp.int32, shape, dim)


def ones_where(condition):
    return jnp.where(condition, 1.0, 0.0).astype(jnp.float32)


def ahead(value, axis):
    return pltpu.roll(value, value.shape[axis] - 1, axis)


def behind(value, axis):
    return pltpu.roll(value, 1, axis)


def sides(shape, width):
    nd = len(shape)
    row = iota(shape, nd - 2)
    col = iota(shape, nd - 1) & (width - 1)
    last_row = row == shape[-2] - 1
    last_col = col == width - 1
    extra = ones_where(row == 0) + ones_where(last_row)
    extra = extra + ones_where(col == 0) + ones_where(last_col)
    return last_row, last_col, extra


def plane_faces(center, edges):
    last_row, last_col, extra = edges
    nd = center.ndim
    north = jnp.where(last_row, 0.0, 0.5 * (center + ahead(center, nd - 2)))
    above = jnp.where(last_col, 0.0, 0.5 * (center + ahead(center, nd - 1)))
    total = north + behind(north, nd - 2) + above + behind(above, nd - 1)
    return north, above, total + center * extra


def plane_sum(field, north, above):
    nd = field.ndim
    total = north * ahead(field, nd - 2) + behind(north * field, nd - 2)
    return total + above * ahead(field, nd - 1) + behind(above * field, nd - 1)


def packed_ahead(wide, width):
    upper, lower = wide[1:], wide[:-1]
    lane = iota(upper.shape, 2)
    return pltpu.roll(jnp.where(lane < width, upper, lower), 128 - width, 2)


def packed_behind(wide, width):
    upper, lower = wide[1:], wide[:-1]
    lane = iota(upper.shape, 2)
    return pltpu.roll(jnp.where(lane >= 128 - width, lower, upper), width, 2)


def packed_faces(wide, width):
    center = wide[1:-1]
    east = 0.5 * (center + packed_ahead(wide, width)[1:])
    west = 0.5 * (center + packed_behind(wide, width)[:-1])
    north, above, total = plane_faces(center, sides(center.shape, width))
    return east, west, north, above, total + east + west


def packed_sum(wide, width, east, west, north, above):
    total = east * packed_ahead(wide, width)[1:] + west * packed_behind(wide, width)[:-1]
    return total + plane_sum(wide[1:-1], north, above)


def kernel(
    spaces,
    shifts,
    residual,
    log_base,
    mask,
    generator,
    point,
    offset,
    table_x,
    table_y,
    table_z,
    amplitude,
    correction,
    mean_field,
    square_field,
    cond,
    rhs,
    face_x,
    face_y,
    face_z,
    diag,
    gain,
    field_a,
    field_b,
    top_halo,
    flags,
    pairs,
    cond_mid,
    rhs_mid,
    mid_halo,
    faces_mid,
    field_mid,
    grown_mid,
    cond_low,
    rhs_low,
    faces_low,
    field_low,
    grown_low,
    arrived,
    copy_sem,
    halo_send,
    halo_recv,
    slab_send,
    slab_recv,
    sum_send,
    sum_recv,
):
    shift = lax.axis_index("shift")
    place = lax.axis_index("space")
    planes, width = log_base.shape[0], log_base.shape[1]
    blocks = mask.shape[0]
    has_left = place > 0
    has_right = place < spaces - 1
    rows = width // shifts

    barrier = pltpu.get_barrier_semaphore()
    near = [(d, place >= d, place < spaces - d) for d in range(1, 4)]
    for d, lower, upper in near:

        @pl.when(lower)
        def _():
            pl.semaphore_signal(barrier, inc=1, device_id={"space": place - d}, device_id_type=MESH)

        @pl.when(upper)
        def _():
            pl.semaphore_signal(barrier, inc=1, device_id={"space": place + d}, device_id_type=MESH)

    for d in range(1, shifts):
        pl.semaphore_signal(
            barrier, inc=1, device_id={"shift": (shift + d) % shifts}, device_id_type=MESH
        )
    own_rhs = pltpu.make_async_copy(residual.at[0], rhs.at[pl.ds(2, planes)], copy_sem)
    own_rhs.start()
    peers = shifts - 1
    for d in range(1, 4):
        peers = peers + (place + spaces - d) // spaces + (2 * spaces - 1 - place - d) // spaces
    pl.semaphore_wait(barrier, peers)

    def exchange(kind, to_left, left_lands, to_right, right_lands):
        leftward = pltpu.make_async_remote_copy(
            src_ref=to_left,
            dst_ref=left_lands,
            send_sem=halo_send.at[kind, 0],
            recv_sem=halo_recv.at[kind, 0],
            device_id={"space": place - 1},
            device_id_type=MESH,
        )
        rightward = pltpu.make_async_remote_copy(
            src_ref=to_right,
            dst_ref=right_lands,
            send_sem=halo_send.at[kind, 1],
            recv_sem=halo_recv.at[kind, 1],
            device_id={"space": place + 1},
            device_id_type=MESH,
        )

        def start():
            pl.when(has_left)(leftward.start)
            pl.when(has_right)(rightward.start)

        def arrive():
            pl.when(has_right)(leftward.wait_recv)
            pl.when(has_left)(rightward.wait_recv)

        def sent():
            pl.when(has_left)(leftward.wait_send)
            pl.when(has_right)(rightward.wait_send)

        return start, arrive, sent

    def spread(kind, slabs):
        made = []
        for d, lower, upper in near:
            leftward = pltpu.make_async_remote_copy(
                src_ref=slabs.at[3],
                dst_ref=slabs.at[3 + d],
                send_sem=slab_send.at[kind, 0, d - 1],
                recv_sem=slab_recv.at[kind, 0, d - 1],
                device_id={"space": place - d},
                device_id_type=MESH,
            )
            rightward = pltpu.make_async_remote_copy(
                src_ref=slabs.at[3],
                dst_ref=slabs.at[3 - d],
                send_sem=slab_send.at[kind, 1, d - 1],
                recv_sem=slab_recv.at[kind, 1, d - 1],
                device_id={"space": place + d},
                device_id_type=MESH,
            )
            made.append((lower, upper, leftward, rightward))

        def start():
            for lower, upper, leftward, rightward in made:
                pl.when(lower)(leftward.start)
                pl.when(upper)(rightward.start)

        def arrive():
            for lower, upper, leftward, rightward in made:
                pl.when(upper)(leftward.wait_recv)
                pl.when(lower)(rightward.wait_recv)

        def sent():
            for lower, upper, leftward, rightward in made:
                pl.when(lower)(leftward.wait_send)
                pl.when(upper)(rightward.wait_send)

        return start, arrive, sent

    end = planes + 2
    rhs_copy = exchange(
        0,
        residual.at[0, pl.ds(0, 2)],
        rhs.at[pl.ds(end, 2)],
        residual.at[0, pl.ds(planes - 2, 2)],
        rhs.at[pl.ds(0, 2)],
    )
    cond_copy = exchange(
        1,
        cond.at[pl.ds(3, 3)],
        cond.at[pl.ds(planes + 3, 3)],
        cond.at[pl.ds(planes, 3)],
        cond.at[pl.ds(0, 3)],
    )
    top_copy = exchange(
        2,
        field_b.at[pl.ds(2, 2)],
        top_halo.at[pl.ds(2, 2)],
        field_b.at[pl.ds(planes, 2)],
        top_halo.at[pl.ds(0, 2)],
    )
    cond_mid_copy = exchange(
        3,
        cond_mid.at[pl.ds(2, 2)],
        cond_mid.at[pl.ds(6, 2)],
        cond_mid.at[pl.ds(4, 2)],
        cond_mid.at[pl.ds(0, 2)],
    )
    rhs_mid_copy = exchange(
        4, rhs_mid.at[1], rhs_mid.at[5], rhs_mid.at[4], rhs_mid.at[0]
    )
    mid_copy = exchange(
        5,
        field_mid.at[pl.ds(1, 2)],
        mid_halo.at[pl.ds(2, 2)],
        field_mid.at[pl.ds(3, 2)],
        mid_halo.at[pl.ds(0, 2)],
    )
    cond_low_copy = spread(0, cond_low)
    rhs_low_copy = spread(1, rhs_low)

    rhs_copy[0]()

    lattice = (point[0] * generator[...]) & (NPTS - 1)
    shifted = lattice.astype(jnp.float32) / NPTS + offset[...]
    fraction = shifted - jnp.floor(shifted)
    weights = amplitude[...] * (1.0 - 2.0 * jnp.abs(2.0 * fraction - 1.0))

    def conductivity(i):
        along = weights * table_x[pl.ds(place * planes + i, 1), :]
        smooth = exact_dot(table_y[...] * along, table_z[...])
        cond[i + 3] = jnp.exp(log_base[i].astype(jnp.float32) + smooth)

    @pl.loop(0, 3)
    def _(i):
        conductivity(i)
        conductivity(planes - 3 + i)

    cond_copy[0]()

    @pl.loop(0, (planes - 6) // 2)
    def _(i):
        conductivity(3 + 2 * i)
        conductivity(4 + 2 * i)

    half = iota((2 * width, 128), 0)
    lane = iota((2 * width, 128), 1)
    gather_mid = ones_where(lane == 64 * (half // 128) + (half & 127) // 2)
    part = iota((4 * 128, 128), 0)
    lane = iota((4 * 128, 128), 1)
    gather_low = ones_where(lane == 32 * (part // 128) + (part & 63) // 2)

    def to_mid(scale):
        folded = []
        for k in range(4):
            pair = [
                pairs[2 * k + h, pl.ds(0, 64, 2), :] + pairs[2 * k + h, pl.ds(1, 64, 2), :]
                for h in range(2)
            ]
            folded.append(jnp.concatenate(pair, axis=1))
        made = scale * exact_dot(jnp.concatenate(folded, axis=0), gather_mid)
        return made.reshape(4, 64, 128)

    def to_low(scale, source, first):
        folded = [
            source[first + q, pl.ds(0, 32, 2), :] + source[first + q, pl.ds(1, 32, 2), :]
            for q in range(4)
        ]
        return scale * exact_dot(jnp.concatenate(folded, axis=1), gather_low)

    @pl.loop(0, planes // 2)
    def _(i):
        pairs[i] = cond[3 + 2 * i] + cond[4 + 2 * i]

    cond_mid[pl.ds(2, 4)] = to_mid(0.125)
    cond_mid_copy[0]()
    cond_low[3] = to_low(0.125, cond_mid, 2)
    cond_low_copy[0]()

    def block(number):
        inside = jnp.where((number >= 0) & (number < blocks), 1.0, 0.0)
        return mask[(number + blocks) % blocks].astype(jnp.float32) * inside

    cols = mask.shape[1]
    up_top = ones_where(iota((width, cols), 0) // 8 == iota((width, cols), 1))
    out_top = ones_where(iota((cols, 128), 1) // 8 == iota((cols, 128), 0))
    up_mid = ones_where(iota((64, cols), 0) // 4 == iota((64, cols), 1))
    out_mid = ones_where((iota((cols, 128), 1) & 63) // 4 == iota((cols, 128), 0))
    up_low = ones_where(iota((32, cols), 0) // 2 == iota((32, cols), 1))
    col = iota((cols, 128), 1)
    out_low = [
        ones_where(((col & 31) // 2 == iota((cols, 128), 0)) & (col // 64 == h)) for h in range(2)
    ]
    active_mid = []
    for k in range(4):
        one = block(2 * place + k - 1)
        flags[k] = flag_dot(flag_dot(up_top, one), out_top)
        active_mid.append(flag_dot(flag_dot(up_mid, one), out_mid))
    active_mid = jnp.stack([active_mid[j] for j in (0, 1, 1, 2, 2, 3)])
    active_low = []
    for s in range(-3, 4):
        parts = [flag_dot(block(2 * (place + s) + h), out_low[h]) for h in range(2)]
        active_low.append(flag_dot(up_low, parts[0] + parts[1]))
    active_low = jnp.stack(active_low)

    own_rhs.wait()
    rhs_copy[1]()
    cond_copy[1]()

    @pl.when(place == 0)
    def _():
        for i in range(3):
            cond[i] = cond[3]
        rhs[pl.ds(0, 2)] = jnp.zeros((2, width, 128), jnp.float32)

    @pl.when(place == spaces - 1)
    def _():
        for i in range(3):
            cond[planes + 3 + i] = cond[planes + 2]
        rhs[pl.ds(end, 2)] = jnp.zeros((2, width, 128), jnp.float32)

    edges = sides((width, 128), 128)

    @pl.loop(0, planes + 4)
    def _(i):
        center = cond[i + 1]
        west = 0.5 * (cond[i] + center)
        east = 0.5 * (center + cond[i + 2])
        north, above, total = plane_faces(center, edges)
        total = total + west + east
        face_x[i] = west
        face_x[i + 1] = east
        face_y[i] = north
        face_z[i] = above
        diag[i] = total
        scale = RELAX * flags[(i + 6) // 8] / total
        gain[i] = scale
        field_a[i] = scale * rhs[i]

    def around(source, i):
        total = face_x[i] * source[i - 1] + face_x[i + 1] * source[i + 1]
        return rhs[i] + total + plane_sum(source[i], face_y[i], face_z[i])

    def swept(source, i):
        kept = (1.0 - RELAX) * flags[(i + 6) // 8] * source[i]
        return kept + gain[i] * around(source, i)

    @pl.loop(1, planes + 3)
    def _(i):
        field_b[i] = swept(field_a, i)

    top_copy[0]()

    def left_over(i):
        return flags[(i + 6) // 8] * (around(field_b, i) - diag[i] * field_b[i])

    @pl.loop(0, planes // 2)
    def _(i):
        pairs[i] = left_over(2 + 2 * i) + left_over(3 + 2 * i)

    rhs_mid[pl.ds(1, 4)] = to_mid(0.5)
    rhs_mid_copy[0]()

    cond_mid_copy[1]()

    @pl.when(place == 0)
    def _():
        outer = pltpu.roll(cond_mid[2], 64, 1)
        cond_mid[0] = outer
        cond_mid[1] = outer

    @pl.when(place == spaces - 1)
    def _():
        outer = pltpu.roll(cond_mid[5], 64, 1)
        cond_mid[6] = outer
        cond_mid[7] = outer

    east, west, north, above, total = packed_faces(cond_mid[...], 64)
    faces_mid[0] = east
    faces_mid[1] = west
    faces_mid[2] = north
    faces_mid[3] = above
    faces_mid[4] = total
    faces_mid[5] = RELAX * active_mid / total
    faces_mid[6] = active_mid

    rhs_mid_copy[1]()

    @pl.when(place == 0)
    def _():
        rhs_mid[0] = jnp.zeros((64, 128), jnp.float32)

    @pl.when(place == spaces - 1)
    def _():
        rhs_mid[5] = jnp.zeros((64, 128), jnp.float32)

    nothing_mid = jnp.zeros((1, 64, 128), jnp.float32)

    def around_mid(wide):
        return rhs_mid[...] + packed_sum(
            wide, 64, faces_mid[0], faces_mid[1], faces_mid[2], faces_mid[3]
        )

    def swept_mid(wide):
        kept = (1.0 - RELAX) * faces_mid[6] * wide[1:-1]
        return kept + faces_mid[5] * around_mid(wide)

    def widened_mid(value):
        return jnp.concatenate([nothing_mid, value, nothing_mid], axis=0)

    solved_mid = swept_mid(widened_mid(faces_mid[5] * rhs_mid[...]))
    field_mid[...] = solved_mid
    mid_copy[0]()
    rest = faces_mid[6] * (around_mid(widened_mid(solved_mid)) - faces_mid[4] * solved_mid)
    grown_mid[pl.ds(0, 6)] = rest
    rhs_low[3] = to_low(0.5, grown_mid, 1)
    rhs_low_copy[0]()

    cond_low_copy[1]()
    for s in (1, 2, 3):

        @pl.when(place < s)
        def _():
            cond_low[3 - s] = pltpu.roll(cond_low[4 - s], 96, 1)

        @pl.when(place >= spaces - s)
        def _():
            cond_low[3 + s] = pltpu.roll(cond_low[2 + s], 32, 1)

    wide = cond_low[...]
    wide = jnp.concatenate([wide[:1], wide, wide[-1:]], axis=0)
    east, west, north, above, total = packed_faces(wide, 32)
    faces_low[0] = east
    faces_low[1] = west
    faces_low[2] = north
    faces_low[3] = above
    faces_low[4] = RELAX * active_low / total
    faces_low[5] = (1.0 - RELAX) * active_low

    rhs_low_copy[1]()
    for s in (1, 2, 3):

        @pl.when(place < s)
        def _():
            rhs_low[3 - s] = jnp.zeros((32, 128), jnp.float32)

        @pl.when(place >= spaces - s)
        def _():
            rhs_low[3 + s] = jnp.zeros((32, 128), jnp.float32)

    nothing_low = jnp.zeros((1, 32, 128), jnp.float32)
    field_low[...] = faces_low[4] * rhs_low[...]

    @pl.loop(0, SWEEPS_LOW - 1)
    def _(step):
        value = field_low[...]
        wide = jnp.concatenate([nothing_low, value, nothing_low], axis=0)
        total = rhs_low[...] + packed_sum(
            wide, 32, faces_low[0], faces_low[1], faces_low[2], faces_low[3]
        )
        field_low[...] = faces_low[5] * value + faces_low[4] * total

    repeat_low = jnp.where(
        iota((128, 4 * 128), 0)
        == 32 * (iota((128, 4 * 128), 1) // 128) + (iota((128, 4 * 128), 1) & 63) // 2,
        1.0,
        0.0,
    ).astype(jnp.float32)
    grown = exact_dot(field_low[pl.ds(2, 3)].reshape(3 * 32, 128), repeat_low)
    for k in range(-2, 6):
        s, q = (k + 4) // 4, (k + 4) % 4
        piece = grown[32 * s : 32 * s + 32, 128 * q : 128 * q + 128]
        grown_mid[k + 2, pl.ds(0, 32, 2), :] = piece
        grown_mid[k + 2, pl.ds(1, 32, 2), :] = piece

    mid_copy[1]()

    @pl.when(place == 0)
    def _():
        mid_halo[pl.ds(0, 2)] = jnp.zeros((2, 64, 128), jnp.float32)

    @pl.when(place == spaces - 1)
    def _():
        mid_halo[pl.ds(2, 2)] = jnp.zeros((2, 64, 128), jnp.float32)

    wide = grown_mid[...] + jnp.concatenate(
        [mid_halo[pl.ds(0, 2)], field_mid[pl.ds(1, 4)], mid_halo[pl.ds(2, 2)]], axis=0
    )
    solved_mid = swept_mid(widened_mid(swept_mid(wide)))

    repeat_mid = jnp.where(
        iota((128, 256), 0) == 64 * (iota((128, 256), 1) // 128) + (iota((128, 256), 1) & 127) // 2,
        1.0,
        0.0,
    ).astype(jnp.float32)
    grown = exact_dot(solved_mid.reshape(6 * 64, 128), repeat_mid)
    for m in range(-1, planes // 2 + 1):
        k, h = (m + 2) // 2, (m + 2) % 2
        piece = grown[64 * k : 64 * k + 64, 128 * h : 128 * h + 128]
        grown_low[m + 1, pl.ds(0, 64, 2), :] = piece
        grown_low[m + 1, pl.ds(1, 64, 2), :] = piece

    top_copy[1]()

    @pl.when(place == 0)
    def _():
        top_halo[pl.ds(0, 2)] = jnp.zeros((2, width, 128), jnp.float32)

    @pl.when(place == spaces - 1)
    def _():
        top_halo[pl.ds(2, 2)] = jnp.zeros((2, width, 128), jnp.float32)

    for i in range(2):
        field_a[i] = top_halo[i] + grown_low[0]
        field_a[end + i] = top_halo[2 + i] + grown_low[planes // 2 + 1]

    @pl.loop(0, planes // 2)
    def _(i):
        piece = grown_low[i + 1]
        field_a[2 + 2 * i] = field_b[2 + 2 * i] + piece
        field_a[3 + 2 * i] = field_b[3 + 2 * i] + piece

    top_copy[2]()

    @pl.loop(1, planes + 3)
    def _(i):
        field_b[i] = swept(field_a, i)

    chunk = planes // GROUPS
    sends = []
    for g in range(GROUPS):

        @pl.loop(0, chunk)
        def _(i):
            correction[0, g * chunk + i] = swept(field_b, g * chunk + i + 2)

        for d in range(1, shifts):
            peer = (shift + d) % shifts
            copy = pltpu.make_async_remote_copy(
                src_ref=correction.at[
                    0, pl.ds(g * chunk, chunk), pl.ds(pl.multiple_of(peer * rows, 8), rows), :
                ],
                dst_ref=arrived.at[d - 1, pl.ds(g * chunk, chunk)],
                send_sem=sum_send.at[d - 1, g],
                recv_sem=sum_recv.at[d - 1, g],
                device_id={"shift": peer},
                device_id_type=MESH,
            )
            copy.start()
            sends.append(copy)

    own_rows = pl.ds(pl.multiple_of(shift * rows, 8), rows)
    for g in range(GROUPS):
        span = pl.ds(g * chunk, chunk)
        value = correction[0, span, own_rows, :]
        total, squares = value, value * value
        for d in range(1, shifts):
            sends[g * (shifts - 1) + d - 1].wait_recv()
            value = arrived[d - 1, span]
            total = total + value
            squares = squares + value * value
        mean_field[span] = total / shifts
        square_field[span] = squares / shifts
    for copy in sends:
        copy.wait_send()
    for group in (rhs_copy, cond_copy, cond_mid_copy, rhs_mid_copy, mid_copy):
        group[2]()
    cond_low_copy[2]()
    rhs_low_copy[2]()


def mode_tables(modes):
    order = np.arange(modes)
    along_x = (order % 4 + 1).astype(np.float64)
    along_y = (order // 4 % 4 + 1).astype(np.float64)
    along_z = (order // 16 + 1).astype(np.float64)
    amplitude = 1.5 / np.sqrt(along_x * along_x + along_y * along_y + along_z * along_z)
    return along_x, along_y, along_z, amplitude


def cosines(frequency, cells):
    position = np.arange(cells) + 0.5
    return np.cos(math.pi * frequency[None, :] * position[:, None] / cells).astype(np.float32)


def local(spaces, shifts, residual, log_base, mask, gen_vector, point_index, shift_values):
    planes, width, depth = log_base.shape
    modes = gen_vector.shape[0]
    along_x, along_y, along_z, amplitude = mode_tables(modes)
    table_x = jnp.asarray(cosines(along_x, planes * spaces))
    table_y = jnp.asarray(cosines(along_y, width))
    table_z = jnp.asarray(np.ascontiguousarray(cosines(along_z, depth).T))
    amplitude = jnp.asarray(amplitude.astype(np.float32)[None])
    rows = width // shifts
    f32 = jnp.float32
    vmem = pl.BlockSpec(memory_space=pltpu.VMEM)

    def top(count):
        return pltpu.VMEM((count, width, depth), f32)

    return pl.pallas_call(
        functools.partial(kernel, spaces, shifts),
        out_shape=(
            jax.ShapeDtypeStruct((1, planes, width, depth), f32),
            jax.ShapeDtypeStruct((planes, rows, depth), f32),
            jax.ShapeDtypeStruct((planes, rows, depth), f32),
        ),
        in_specs=[
            pl.BlockSpec(memory_space=pl.ANY),
            vmem,
            vmem,
            vmem,
            pl.BlockSpec(memory_space=pltpu.SMEM),
            vmem,
            vmem,
            vmem,
            vmem,
            vmem,
        ],
        out_specs=(vmem, vmem, vmem),
        scratch_shapes=[
            top(planes + 6),
            top(planes + 4),
            top(planes + 5),
            top(planes + 4),
            top(planes + 4),
            top(planes + 4),
            top(planes + 4),
            top(planes + 4),
            top(planes + 4),
            top(4),
            top(4),
            top(planes // 2),
            pltpu.VMEM((8, 64, 128), f32),
            pltpu.VMEM((6, 64, 128), f32),
            pltpu.VMEM((4, 64, 128), f32),
            pltpu.VMEM((7, 6, 64, 128), f32),
            pltpu.VMEM((6, 64, 128), f32),
            pltpu.VMEM((8, 64, 128), f32),
            pltpu.VMEM((7, 32, 128), f32),
            pltpu.VMEM((7, 32, 128), f32),
            pltpu.VMEM((6, 7, 32, 128), f32),
            pltpu.VMEM((7, 32, 128), f32),
            top(planes // 2 + 2),
            pltpu.VMEM((shifts - 1, planes, rows, depth), f32),
            pltpu.SemaphoreType.DMA,
            pltpu.SemaphoreType.DMA((6, 2)),
            pltpu.SemaphoreType.DMA((6, 2)),
            pltpu.SemaphoreType.DMA((2, 2, 3)),
            pltpu.SemaphoreType.DMA((2, 2, 3)),
            pltpu.SemaphoreType.DMA((shifts - 1, GROUPS)),
            pltpu.SemaphoreType.DMA((shifts - 1, GROUPS)),
        ],
        compiler_params=pltpu.CompilerParams(
            collective_id=0, has_side_effects=True, vmem_limit_bytes=48 * 1024 * 1024
        ),
        name="cycle",
    )(
        residual,
        log_base,
        mask,
        gen_vector[None],
        point_index,
        shift_values,
        table_x,
        table_y,
        table_z,
        amplitude,
    )


def solution(mesh):
    placed = (
        P("shift", "space", None, None),
        P("space", None, None),
        P(),
        P(),
        P("shift"),
        P("shift", None),
    )
    return jax.shard_map(
        functools.partial(local, mesh.shape["space"], mesh.shape["shift"]),
        mesh=mesh,
        in_specs=placed,
        out_specs=(
            P("shift", "space", None, None),
            P("space", "shift", None),
            P("space", "shift", None),
        ),
        check_vma=False,
    )
```

```python
import functools
import math

import jax
import jax.numpy as jnp
import numpy as np
from jax import lax
from jax.experimental import pallas as pl
from jax.experimental.pallas import tpu as pltpu
from jax.sharding import PartitionSpec as P

NPTS = 1024
SWEEPS_LOW = 8
RELAX = 0.8
HBM = pltpu.HBM
MESH = pl.DeviceIdType.MESH
HIGHEST = lax.Precision.HIGHEST
GROUPS = 4


def exact_dot(a, b):
    return jnp.dot(a, b, precision=HIGHEST, preferred_element_type=jnp.float32)


def flag_dot(a, b):
    return jnp.dot(
        a.astype(jnp.bfloat16), b.astype(jnp.bfloat16), preferred_element_type=jnp.float32
    )


def iota(shape, dim):
    return lax.broadcasted_iota(jnp.int32, shape, dim)


def ones_where(condition):
    return jnp.where(condition, 1.0, 0.0).astype(jnp.float32)


def ahead(value, axis):
    return pltpu.roll(value, value.shape[axis] - 1, axis)


def behind(value, axis):
    return pltpu.roll(value, 1, axis)


def sides(shape, width):
    nd = len(shape)
    row = iota(shape, nd - 2)
    col = iota(shape, nd - 1) & (width - 1)
    last_row = row == shape[-2] - 1
    last_col = col == width - 1
    extra = ones_where(row == 0) + ones_where(last_row)
    extra = extra + ones_where(col == 0) + ones_where(last_col)
    return last_row, last_col, extra


def plane_faces(center, edges):
    last_row, last_col, extra = edges
    nd = center.ndim
    north = jnp.where(last_row, 0.0, 0.5 * (center + ahead(center, nd - 2)))
    above = jnp.where(last_col, 0.0, 0.5 * (center + ahead(center, nd - 1)))
    total = north + behind(north, nd - 2) + above + behind(above, nd - 1)
    return north, above, total + center * extra


def plane_sum(field, north, above):
    nd = field.ndim
    total = north * ahead(field, nd - 2) + behind(north * field, nd - 2)
    return total + above * ahead(field, nd - 1) + behind(above * field, nd - 1)


def packed_ahead(wide, width):
    upper, lower = wide[1:], wide[:-1]
    lane = iota(upper.shape, 2)
    return pltpu.roll(jnp.where(lane < width, upper, lower), 128 - width, 2)


def packed_behind(wide, width):
    upper, lower = wide[1:], wide[:-1]
    lane = iota(upper.shape, 2)
    return pltpu.roll(jnp.where(lane >= 128 - width, lower, upper), width, 2)


def packed_faces(wide, width):
    center = wide[1:-1]
    east = 0.5 * (center + packed_ahead(wide, width)[1:])
    west = 0.5 * (center + packed_behind(wide, width)[:-1])
    north, above, total = plane_faces(center, sides(center.shape, width))
    return east, west, north, above, total + east + west


def packed_sum(wide, width, east, west, north, above):
    total = east * packed_ahead(wide, width)[1:] + west * packed_behind(wide, width)[:-1]
    return total + plane_sum(wide[1:-1], north, above)


def kernel(
    spaces,
    shifts,
    residual,
    *refs,
):
    sources, refs = refs[:9], refs[9:]
    run(spaces, shifts, residual, sources, *refs)


def run(
    spaces,
    shifts,
    residual,
    sources,
    correction,
    mean_field,
    square_field,
    cond,
    rhs,
    face_x,
    face_y,
    face_z,
    diag,
    gain,
    field_a,
    field_b,
    top_halo,
    flags,
    pairs,
    cond_mid,
    rhs_mid,
    mid_halo,
    faces_mid,
    field_mid,
    grown_mid,
    cond_low,
    rhs_low,
    faces_low,
    field_low,
    grown_low,
    arrived,
    log_base,
    mask,
    generator,
    point,
    offset,
    table_x,
    table_y,
    table_z,
    amplitude,
    copy_sem,
    halo_send,
    halo_recv,
    slab_send,
    slab_recv,
    sum_send,
    sum_recv,
):
    shift = lax.axis_index("shift")
    place = lax.axis_index("space")
    planes, width = log_base.shape[0], log_base.shape[1]
    blocks = mask.shape[0]
    has_left = place > 0
    has_right = place < spaces - 1
    rows = width // shifts

    held = (log_base, mask, generator, point, offset, table_x, table_y, table_z, amplitude)
    fetches = [
        pltpu.make_async_copy(source, target, copy_sem.at[n])
        for n, (source, target) in enumerate(zip(sources, held))
    ]
    own_rhs = pltpu.make_async_copy(residual.at[0], rhs.at[pl.ds(2, planes)], copy_sem.at[9])
    for fetch in fetches:
        fetch.start()
    own_rhs.start()
    barrier = pltpu.get_barrier_semaphore()
    near = [(d, place >= d, place < spaces - d) for d in range(1, 4)]
    for d, lower, upper in near:

        @pl.when(lower)
        def _():
            pl.semaphore_signal(barrier, inc=1, device_id={"space": place - d}, device_id_type=MESH)

        @pl.when(upper)
        def _():
            pl.semaphore_signal(barrier, inc=1, device_id={"space": place + d}, device_id_type=MESH)

    for d in range(1, shifts):
        pl.semaphore_signal(
            barrier, inc=1, device_id={"shift": (shift + d) % shifts}, device_id_type=MESH
        )
    peers = shifts - 1
    for d in range(1, 4):
        peers = peers + (place + spaces - d) // spaces + (2 * spaces - 1 - place - d) // spaces
    pl.semaphore_wait(barrier, peers)

    def exchange(kind, to_left, left_lands, to_right, right_lands):
        leftward = pltpu.make_async_remote_copy(
            src_ref=to_left,
            dst_ref=left_lands,
            send_sem=halo_send.at[kind, 0],
            recv_sem=halo_recv.at[kind, 0],
            device_id={"space": place - 1},
            device_id_type=MESH,
        )
        rightward = pltpu.make_async_remote_copy(
            src_ref=to_right,
            dst_ref=right_lands,
            send_sem=halo_send.at[kind, 1],
            recv_sem=halo_recv.at[kind, 1],
            device_id={"space": place + 1},
            device_id_type=MESH,
        )

        def start():
            pl.when(has_left)(leftward.start)
            pl.when(has_right)(rightward.start)

        def arrive():
            pl.when(has_right)(leftward.wait_recv)
            pl.when(has_left)(rightward.wait_recv)

        def sent():
            pl.when(has_left)(leftward.wait_send)
            pl.when(has_right)(rightward.wait_send)

        return start, arrive, sent

    def spread(kind, slabs):
        made = []
        for d, lower, upper in near:
            leftward = pltpu.make_async_remote_copy(
                src_ref=slabs.at[3],
                dst_ref=slabs.at[3 + d],
                send_sem=slab_send.at[kind, 0, d - 1],
                recv_sem=slab_recv.at[kind, 0, d - 1],
                device_id={"space": place - d},
                device_id_type=MESH,
            )
            rightward = pltpu.make_async_remote_copy(
                src_ref=slabs.at[3],
                dst_ref=slabs.at[3 - d],
                send_sem=slab_send.at[kind, 1, d - 1],
                recv_sem=slab_recv.at[kind, 1, d - 1],
                device_id={"space": place + d},
                device_id_type=MESH,
            )
            made.append((lower, upper, leftward, rightward))

        def start():
            for lower, upper, leftward, rightward in made:
                pl.when(lower)(leftward.start)
                pl.when(upper)(rightward.start)

        def arrive():
            for lower, upper, leftward, rightward in made:
                pl.when(upper)(leftward.wait_recv)
                pl.when(lower)(rightward.wait_recv)

        def sent():
            for lower, upper, leftward, rightward in made:
                pl.when(lower)(leftward.wait_send)
                pl.when(upper)(rightward.wait_send)

        return start, arrive, sent

    end = planes + 2
    rhs_copy = exchange(
        0,
        residual.at[0, pl.ds(0, 2)],
        rhs.at[pl.ds(end, 2)],
        residual.at[0, pl.ds(planes - 2, 2)],
        rhs.at[pl.ds(0, 2)],
    )
    cond_copy = exchange(
        1,
        cond.at[pl.ds(3, 3)],
        cond.at[pl.ds(planes + 3, 3)],
        cond.at[pl.ds(planes, 3)],
        cond.at[pl.ds(0, 3)],
    )
    top_copy = exchange(
        2,
        field_b.at[pl.ds(2, 2)],
        top_halo.at[pl.ds(2, 2)],
        field_b.at[pl.ds(planes, 2)],
        top_halo.at[pl.ds(0, 2)],
    )
    cond_mid_copy = exchange(
        3,
        cond_mid.at[pl.ds(2, 2)],
        cond_mid.at[pl.ds(6, 2)],
        cond_mid.at[pl.ds(4, 2)],
        cond_mid.at[pl.ds(0, 2)],
    )
    rhs_mid_copy = exchange(
        4, rhs_mid.at[1], rhs_mid.at[5], rhs_mid.at[4], rhs_mid.at[0]
    )
    mid_copy = exchange(
        5,
        field_mid.at[pl.ds(1, 2)],
        mid_halo.at[pl.ds(2, 2)],
        field_mid.at[pl.ds(3, 2)],
        mid_halo.at[pl.ds(0, 2)],
    )
    cond_low_copy = spread(0, cond_low)
    rhs_low_copy = spread(1, rhs_low)

    rhs_copy[0]()
    for fetch in fetches:
        fetch.wait()

    lattice = (point[...] * generator[...]) & (NPTS - 1)
    shifted = lattice.astype(jnp.float32) / NPTS + offset[...]
    fraction = shifted - jnp.floor(shifted)
    weights = amplitude[...] * (1.0 - 2.0 * jnp.abs(2.0 * fraction - 1.0))

    def conductivity(i):
        along = weights * table_x[pl.ds(place * planes + i, 1), :]
        smooth = exact_dot(table_y[...] * along, table_z[...])
        cond[i + 3] = jnp.exp(log_base[i].astype(jnp.float32) + smooth)

    @pl.loop(0, 3)
    def _(i):
        conductivity(i)
        conductivity(planes - 3 + i)

    cond_copy[0]()

    @pl.loop(0, (planes - 6) // 2)
    def _(i):
        conductivity(3 + 2 * i)
        conductivity(4 + 2 * i)

    half = iota((2 * width, 128), 0)
    lane = iota((2 * width, 128), 1)
    gather_mid = ones_where(lane == 64 * (half // 128) + (half & 127) // 2)
    part = iota((4 * 128, 128), 0)
    lane = iota((4 * 128, 128), 1)
    gather_low = ones_where(lane == 32 * (part // 128) + (part & 63) // 2)

    def to_mid(scale):
        folded = []
        for k in range(4):
            pair = [
                pairs[2 * k + h, pl.ds(0, 64, 2), :] + pairs[2 * k + h, pl.ds(1, 64, 2), :]
                for h in range(2)
            ]
            folded.append(jnp.concatenate(pair, axis=1))
        made = scale * exact_dot(jnp.concatenate(folded, axis=0), gather_mid)
        return made.reshape(4, 64, 128)

    def to_low(scale, source, first):
        folded = [
            source[first + q, pl.ds(0, 32, 2), :] + source[first + q, pl.ds(1, 32, 2), :]
            for q in range(4)
        ]
        return scale * exact_dot(jnp.concatenate(folded, axis=1), gather_low)

    @pl.loop(0, planes // 2)
    def _(i):
        pairs[i] = cond[3 + 2 * i] + cond[4 + 2 * i]

    cond_mid[pl.ds(2, 4)] = to_mid(0.125)
    cond_mid_copy[0]()
    cond_low[3] = to_low(0.125, cond_mid, 2)
    cond_low_copy[0]()

    def block(number):
        inside = jnp.where((number >= 0) & (number < blocks), 1.0, 0.0)
        return mask[(number + blocks) % blocks].astype(jnp.float32) * inside

    cols = mask.shape[1]
    up_top = ones_where(iota((width, cols), 0) // 8 == iota((width, cols), 1))
    out_top = ones_where(iota((cols, 128), 1) // 8 == iota((cols, 128), 0))
    up_mid = ones_where(iota((64, cols), 0) // 4 == iota((64, cols), 1))
    out_mid = ones_where((iota((cols, 128), 1) & 63) // 4 == iota((cols, 128), 0))
    up_low = ones_where(iota((32, cols), 0) // 2 == iota((32, cols), 1))
    col = iota((cols, 128), 1)
    out_low = [
        ones_where(((col & 31) // 2 == iota((cols, 128), 0)) & (col // 64 == h)) for h in range(2)
    ]
    active_mid = []
    for k in range(4):
        one = block(2 * place + k - 1)
        flags[k] = flag_dot(flag_dot(up_top, one), out_top)
        active_mid.append(flag_dot(flag_dot(up_mid, one), out_mid))
    active_mid = jnp.stack([active_mid[j] for j in (0, 1, 1, 2, 2, 3)])
    active_low = []
    for s in range(-3, 4):
        parts = [flag_dot(block(2 * (place + s) + h), out_low[h]) for h in range(2)]
        active_low.append(flag_dot(up_low, parts[0] + parts[1]))
    active_low = jnp.stack(active_low)

    own_rhs.wait()
    edges = sides((width, 128), 128)

    def weigh(i):
        center = cond[i + 1]
        west = 0.5 * (cond[i] + center)
        east = 0.5 * (center + cond[i + 2])
        north, above, total = plane_faces(center, edges)
        total = total + west + east
        face_x[i] = west
        face_x[i + 1] = east
        face_y[i] = north
        face_z[i] = above
        diag[i] = total
        scale = RELAX * flags[(i + 6) // 8] / total
        gain[i] = scale
        field_a[i] = scale * rhs[i]

    def around(source, i):
        total = face_x[i] * source[i - 1] + face_x[i + 1] * source[i + 1]
        return rhs[i] + total + plane_sum(source[i], face_y[i], face_z[i])

    def swept(source, i):
        kept = (1.0 - RELAX) * flags[(i + 6) // 8] * source[i]
        return kept + gain[i] * around(source, i)

    pl.loop(3, planes + 1, unroll=2)(weigh)

    @pl.loop(4, planes, unroll=2)
    def _(i):
        field_b[i] = swept(field_a, i)

    rhs_copy[1]()
    cond_copy[1]()

    @pl.when(place == 0)
    def _():
        for i in range(3):
            cond[i] = cond[3]
        rhs[pl.ds(0, 2)] = jnp.zeros((2, width, 128), jnp.float32)

    @pl.when(place == spaces - 1)
    def _():
        for i in range(3):
            cond[planes + 3 + i] = cond[planes + 2]
        rhs[pl.ds(end, 2)] = jnp.zeros((2, width, 128), jnp.float32)

    @pl.loop(0, 3)
    def _(i):
        weigh(i)
        weigh(planes + 1 + i)

    @pl.loop(0, 3)
    def _(i):
        field_b[1 + i] = swept(field_a, 1 + i)
        field_b[planes + i] = swept(field_a, planes + i)

    top_copy[0]()

    def left_over(i):
        return flags[(i + 6) // 8] * (around(field_b, i) - diag[i] * field_b[i])

    @pl.loop(0, planes // 2)
    def _(i):
        pairs[i] = left_over(2 + 2 * i) + left_over(3 + 2 * i)

    rhs_mid[pl.ds(1, 4)] = to_mid(0.5)
    rhs_mid_copy[0]()

    cond_mid_copy[1]()

    @pl.when(place == 0)
    def _():
        outer = pltpu.roll(cond_mid[2], 64, 1)
        cond_mid[0] = outer
        cond_mid[1] = outer

    @pl.when(place == spaces - 1)
    def _():
        outer = pltpu.roll(cond_mid[5], 64, 1)
        cond_mid[6] = outer
        cond_mid[7] = outer

    east, west, north, above, total = packed_faces(cond_mid[...], 64)
    faces_mid[0] = east
    faces_mid[1] = west
    faces_mid[2] = north
    faces_mid[3] = above
    faces_mid[4] = total
    faces_mid[5] = RELAX * active_mid / total
    faces_mid[6] = active_mid

    rhs_mid_copy[1]()

    @pl.when(place == 0)
    def _():
        rhs_mid[0] = jnp.zeros((64, 128), jnp.float32)

    @pl.when(place == spaces - 1)
    def _():
        rhs_mid[5] = jnp.zeros((64, 128), jnp.float32)

    nothing_mid = jnp.zeros((1, 64, 128), jnp.float32)

    def around_mid(wide):
        return rhs_mid[...] + packed_sum(
            wide, 64, faces_mid[0], faces_mid[1], faces_mid[2], faces_mid[3]
        )

    def swept_mid(wide):
        kept = (1.0 - RELAX) * faces_mid[6] * wide[1:-1]
        return kept + faces_mid[5] * around_mid(wide)

    def widened_mid(value):
        return jnp.concatenate([nothing_mid, value, nothing_mid], axis=0)

    solved_mid = swept_mid(widened_mid(faces_mid[5] * rhs_mid[...]))
    field_mid[...] = solved_mid
    mid_copy[0]()
    rest = faces_mid[6] * (around_mid(widened_mid(solved_mid)) - faces_mid[4] * solved_mid)
    grown_mid[pl.ds(0, 6)] = rest
    rhs_low[3] = to_low(0.5, grown_mid, 1)
    rhs_low_copy[0]()

    cond_low_copy[1]()
    for s in (1, 2, 3):

        @pl.when(place < s)
        def _():
            cond_low[3 - s] = pltpu.roll(cond_low[4 - s], 96, 1)

        @pl.when(place >= spaces - s)
        def _():
            cond_low[3 + s] = pltpu.roll(cond_low[2 + s], 32, 1)

    wide = cond_low[...]
    wide = jnp.concatenate([wide[:1], wide, wide[-1:]], axis=0)
    east, west, north, above, total = packed_faces(wide, 32)
    faces_low[0] = east
    faces_low[1] = west
    faces_low[2] = north
    faces_low[3] = above
    faces_low[4] = RELAX * active_low / total
    faces_low[5] = (1.0 - RELAX) * active_low

    rhs_low_copy[1]()
    for s in (1, 2, 3):

        @pl.when(place < s)
        def _():
            rhs_low[3 - s] = jnp.zeros((32, 128), jnp.float32)

        @pl.when(place >= spaces - s)
        def _():
            rhs_low[3 + s] = jnp.zeros((32, 128), jnp.float32)

    nothing_low = jnp.zeros((1, 32, 128), jnp.float32)
    field_low[...] = faces_low[4] * rhs_low[...]

    @pl.loop(0, SWEEPS_LOW - 1)
    def _(step):
        value = field_low[...]
        wide = jnp.concatenate([nothing_low, value, nothing_low], axis=0)
        total = rhs_low[...] + packed_sum(
            wide, 32, faces_low[0], faces_low[1], faces_low[2], faces_low[3]
        )
        field_low[...] = faces_low[5] * value + faces_low[4] * total

    repeat_low = jnp.where(
        iota((128, 4 * 128), 0)
        == 32 * (iota((128, 4 * 128), 1) // 128) + (iota((128, 4 * 128), 1) & 63) // 2,
        1.0,
        0.0,
    ).astype(jnp.float32)
    grown = exact_dot(field_low[pl.ds(2, 3)].reshape(3 * 32, 128), repeat_low)
    for k in range(-2, 6):
        s, q = (k + 4) // 4, (k + 4) % 4
        piece = grown[32 * s : 32 * s + 32, 128 * q : 128 * q + 128]
        grown_mid[k + 2, pl.ds(0, 32, 2), :] = piece
        grown_mid[k + 2, pl.ds(1, 32, 2), :] = piece

    mid_copy[1]()

    @pl.when(place == 0)
    def _():
        mid_halo[pl.ds(0, 2)] = jnp.zeros((2, 64, 128), jnp.float32)

    @pl.when(place == spaces - 1)
    def _():
        mid_halo[pl.ds(2, 2)] = jnp.zeros((2, 64, 128), jnp.float32)

    wide = grown_mid[...] + jnp.concatenate(
        [mid_halo[pl.ds(0, 2)], field_mid[pl.ds(1, 4)], mid_halo[pl.ds(2, 2)]], axis=0
    )
    solved_mid = swept_mid(widened_mid(swept_mid(wide)))

    repeat_mid = jnp.where(
        iota((128, 256), 0) == 64 * (iota((128, 256), 1) // 128) + (iota((128, 256), 1) & 127) // 2,
        1.0,
        0.0,
    ).astype(jnp.float32)
    grown = exact_dot(solved_mid.reshape(6 * 64, 128), repeat_mid)
    for m in range(-1, planes // 2 + 1):
        k, h = (m + 2) // 2, (m + 2) % 2
        piece = grown[64 * k : 64 * k + 64, 128 * h : 128 * h + 128]
        grown_low[m + 1, pl.ds(0, 64, 2), :] = piece
        grown_low[m + 1, pl.ds(1, 64, 2), :] = piece

    top_copy[1]()

    @pl.when(place == 0)
    def _():
        top_halo[pl.ds(0, 2)] = jnp.zeros((2, width, 128), jnp.float32)

    @pl.when(place == spaces - 1)
    def _():
        top_halo[pl.ds(2, 2)] = jnp.zeros((2, width, 128), jnp.float32)

    for i in range(2):
        field_a[i] = top_halo[i] + grown_low[0]
        field_a[end + i] = top_halo[2 + i] + grown_low[planes // 2 + 1]

    @pl.loop(0, planes // 2)
    def _(i):
        piece = grown_low[i + 1]
        field_a[2 + 2 * i] = field_b[2 + 2 * i] + piece
        field_a[3 + 2 * i] = field_b[3 + 2 * i] + piece

    top_copy[2]()

    @pl.loop(1, planes + 3, unroll=2)
    def _(i):
        field_b[i] = swept(field_a, i)

    chunk = planes // GROUPS
    sends = []
    for g in range(GROUPS):

        @pl.loop(0, chunk, unroll=2)
        def _(i):
            correction[0, g * chunk + i] = swept(field_b, g * chunk + i + 2)

        for d in range(1, shifts):
            peer = (shift + d) % shifts
            copy = pltpu.make_async_remote_copy(
                src_ref=correction.at[
                    0, pl.ds(g * chunk, chunk), pl.ds(pl.multiple_of(peer * rows, 8), rows), :
                ],
                dst_ref=arrived.at[d - 1, pl.ds(g * chunk, chunk)],
                send_sem=sum_send.at[d - 1, g],
                recv_sem=sum_recv.at[d - 1, g],
                device_id={"shift": peer},
                device_id_type=MESH,
            )
            copy.start()
            sends.append(copy)

    own_rows = pl.ds(pl.multiple_of(shift * rows, 8), rows)
    for g in range(GROUPS):
        span = pl.ds(g * chunk, chunk)
        value = correction[0, span, own_rows, :]
        total, squares = value, value * value
        for d in range(1, shifts):
            sends[g * (shifts - 1) + d - 1].wait_recv()
            value = arrived[d - 1, span]
            total = total + value
            squares = squares + value * value
        mean_field[span] = total / shifts
        square_field[span] = squares / shifts
    for copy in sends:
        copy.wait_send()
    for group in (rhs_copy, cond_copy, cond_mid_copy, rhs_mid_copy, mid_copy):
        group[2]()
    cond_low_copy[2]()
    rhs_low_copy[2]()


def mode_tables(modes):
    order = np.arange(modes)
    along_x = (order % 4 + 1).astype(np.float64)
    along_y = (order // 4 % 4 + 1).astype(np.float64)
    along_z = (order // 16 + 1).astype(np.float64)
    amplitude = 1.5 / np.sqrt(along_x * along_x + along_y * along_y + along_z * along_z)
    return along_x, along_y, along_z, amplitude


def cosines(frequency, cells):
    position = np.arange(cells) + 0.5
    return np.cos(math.pi * frequency[None, :] * position[:, None] / cells).astype(np.float32)


def local(spaces, shifts, residual, log_base, mask, gen_vector, point_index, shift_values):
    planes, width, depth = log_base.shape
    modes = gen_vector.shape[0]
    along_x, along_y, along_z, amplitude = mode_tables(modes)
    table_x = jnp.asarray(cosines(along_x, planes * spaces))
    table_y = jnp.asarray(cosines(along_y, width))
    table_z = jnp.asarray(np.ascontiguousarray(cosines(along_z, depth).T))
    amplitude = jnp.asarray(amplitude.astype(np.float32)[None])
    rows = width // shifts
    f32 = jnp.float32
    vmem = pl.BlockSpec(memory_space=pltpu.VMEM)

    def top(count):
        return pltpu.VMEM((count, width, depth), f32)

    small = (
        log_base,
        mask,
        gen_vector[None],
        point_index[None],
        shift_values,
        table_x,
        table_y,
        table_z,
        amplitude,
    )
    return pl.pallas_call(
        functools.partial(kernel, spaces, shifts),
        out_shape=(
            jax.ShapeDtypeStruct((1, planes, width, depth), f32),
            jax.ShapeDtypeStruct((planes, rows, depth), f32),
            jax.ShapeDtypeStruct((planes, rows, depth), f32),
        ),
        in_specs=[pl.BlockSpec(memory_space=HBM)] * (1 + len(small)),
        out_specs=(vmem, vmem, vmem),
        scratch_shapes=[
            top(planes + 6),
            top(planes + 4),
            top(planes + 5),
            top(planes + 4),
            top(planes + 4),
            top(planes + 4),
            top(planes + 4),
            top(planes + 4),
            top(planes + 4),
            top(4),
            top(4),
            top(planes // 2),
            pltpu.VMEM((8, 64, 128), f32),
            pltpu.VMEM((6, 64, 128), f32),
            pltpu.VMEM((4, 64, 128), f32),
            pltpu.VMEM((7, 6, 64, 128), f32),
            pltpu.VMEM((6, 64, 128), f32),
            pltpu.VMEM((8, 64, 128), f32),
            pltpu.VMEM((7, 32, 128), f32),
            pltpu.VMEM((7, 32, 128), f32),
            pltpu.VMEM((6, 7, 32, 128), f32),
            pltpu.VMEM((7, 32, 128), f32),
            top(planes // 2 + 2),
            pltpu.VMEM((shifts - 1, planes, rows, depth), f32),
            *[pltpu.VMEM(array.shape, array.dtype) for array in small],
            pltpu.SemaphoreType.DMA((10,)),
            pltpu.SemaphoreType.DMA((6, 2)),
            pltpu.SemaphoreType.DMA((6, 2)),
            pltpu.SemaphoreType.DMA((2, 2, 3)),
            pltpu.SemaphoreType.DMA((2, 2, 3)),
            pltpu.SemaphoreType.DMA((shifts - 1, GROUPS)),
            pltpu.SemaphoreType.DMA((shifts - 1, GROUPS)),
        ],
        compiler_params=pltpu.CompilerParams(
            collective_id=0, has_side_effects=True, vmem_limit_bytes=63 * 1024 * 1024
        ),
        name="cycle",
    )(
        residual,
        *small,
    )


def solution(mesh):
    placed = (
        P("shift", "space", None, None),
        P("space", None, None),
        P(),
        P(),
        P("shift"),
        P("shift", None),
    )
    return jax.shard_map(
        functools.partial(local, mesh.shape["space"], mesh.shape["shift"]),
        mesh=mesh,
        in_specs=placed,
        out_specs=(
            P("shift", "space", None, None),
            P("space", "shift", None),
            P("space", "shift", None),
        ),
        check_vma=False,
    )
```

```python
import functools
import math

import jax
import jax.numpy as jnp
import numpy as np
from jax import lax
from jax.experimental import pallas as pl
from jax.experimental.pallas import tpu as pltpu
from jax.sharding import PartitionSpec as P

NPTS = 1024
SWEEPS_LOW = 8
RELAX = 0.8
HBM = pltpu.HBM
MESH = pl.DeviceIdType.MESH
HIGHEST = lax.Precision.HIGHEST
GROUPS = 8


def exact_dot(a, b):
    return jnp.dot(a, b, precision=HIGHEST, preferred_element_type=jnp.float32)


def flag_dot(a, b):
    return jnp.dot(
        a.astype(jnp.bfloat16), b.astype(jnp.bfloat16), preferred_element_type=jnp.float32
    )


def iota(shape, dim):
    return lax.broadcasted_iota(jnp.int32, shape, dim)


def ones_where(condition):
    return jnp.where(condition, 1.0, 0.0).astype(jnp.float32)


def ahead(value, axis):
    return pltpu.roll(value, value.shape[axis] - 1, axis)


def behind(value, axis):
    return pltpu.roll(value, 1, axis)


def sides(shape, width):
    nd = len(shape)
    row = iota(shape, nd - 2)
    col = iota(shape, nd - 1) & (width - 1)
    last_row = row == shape[-2] - 1
    last_col = col == width - 1
    extra = ones_where(row == 0) + ones_where(last_row)
    extra = extra + ones_where(col == 0) + ones_where(last_col)
    return last_row, last_col, extra


def plane_faces(center, edges):
    last_row, last_col, extra = edges
    nd = center.ndim
    north = jnp.where(last_row, 0.0, 0.5 * (center + ahead(center, nd - 2)))
    above = jnp.where(last_col, 0.0, 0.5 * (center + ahead(center, nd - 1)))
    total = north + behind(north, nd - 2) + above + behind(above, nd - 1)
    return north, above, total + center * extra


def plane_sum(field, north, above):
    nd = field.ndim
    total = north * ahead(field, nd - 2) + behind(north * field, nd - 2)
    return total + above * ahead(field, nd - 1) + behind(above * field, nd - 1)


def packed_ahead(wide, width):
    upper, lower = wide[1:], wide[:-1]
    lane = iota(upper.shape, 2)
    return pltpu.roll(jnp.where(lane < width, upper, lower), 128 - width, 2)


def packed_behind(wide, width):
    upper, lower = wide[1:], wide[:-1]
    lane = iota(upper.shape, 2)
    return pltpu.roll(jnp.where(lane >= 128 - width, lower, upper), width, 2)


def packed_faces(wide, width):
    center = wide[1:-1]
    east = 0.5 * (center + packed_ahead(wide, width)[1:])
    west = 0.5 * (center + packed_behind(wide, width)[:-1])
    north, above, total = plane_faces(center, sides(center.shape, width))
    return east, west, north, above, total + east + west


def packed_sum(wide, width, east, west, north, above):
    total = east * packed_ahead(wide, width)[1:] + west * packed_behind(wide, width)[:-1]
    return total + plane_sum(wide[1:-1], north, above)


def kernel(
    spaces,
    shifts,
    residual,
    *refs,
):
    sources, refs = refs[:9], refs[9:]
    run(spaces, shifts, residual, sources, *refs)


def run(
    spaces,
    shifts,
    residual,
    sources,
    handed,
    mean_field,
    square_field,
    cond,
    rhs,
    face_x,
    face_y,
    face_z,
    diag,
    gain,
    field_a,
    field_b,
    top_halo,
    flags,
    pairs,
    cond_mid,
    rhs_mid,
    mid_halo,
    faces_mid,
    field_mid,
    grown_mid,
    cond_low,
    rhs_low,
    faces_low,
    field_low,
    grown_low,
    arrived,
    correction,
    log_base,
    mask,
    generator,
    point,
    offset,
    table_x,
    table_y,
    table_z,
    amplitude,
    copy_sem,
    halo_send,
    halo_recv,
    slab_send,
    slab_recv,
    sum_send,
    sum_recv,
):
    shift = lax.axis_index("shift")
    place = lax.axis_index("space")
    planes, width = log_base.shape[0], log_base.shape[1]
    blocks = mask.shape[0]
    has_left = place > 0
    has_right = place < spaces - 1
    rows = width // shifts

    held = (log_base, mask, generator, point, offset, table_x, table_y, table_z, amplitude)
    fetches = [
        pltpu.make_async_copy(source, target, copy_sem.at[n])
        for n, (source, target) in enumerate(zip(sources, held))
    ]
    own_rhs = pltpu.make_async_copy(residual.at[0], rhs.at[pl.ds(2, planes)], copy_sem.at[9])
    for fetch in fetches:
        fetch.start()
    own_rhs.start()
    barrier = pltpu.get_barrier_semaphore()
    near = [(d, place >= d, place < spaces - d) for d in range(1, 4)]
    for d, lower, upper in near:

        @pl.when(lower)
        def _():
            pl.semaphore_signal(barrier, inc=1, device_id={"space": place - d}, device_id_type=MESH)

        @pl.when(upper)
        def _():
            pl.semaphore_signal(barrier, inc=1, device_id={"space": place + d}, device_id_type=MESH)

    for d in range(1, shifts):
        pl.semaphore_signal(
            barrier, inc=1, device_id={"shift": (shift + d) % shifts}, device_id_type=MESH
        )
    peers = shifts - 1
    for d in range(1, 4):
        peers = peers + (place + spaces - d) // spaces + (2 * spaces - 1 - place - d) // spaces
    pl.semaphore_wait(barrier, peers)

    def exchange(kind, to_left, left_lands, to_right, right_lands):
        leftward = pltpu.make_async_remote_copy(
            src_ref=to_left,
            dst_ref=left_lands,
            send_sem=halo_send.at[kind, 0],
            recv_sem=halo_recv.at[kind, 0],
            device_id={"space": place - 1},
            device_id_type=MESH,
        )
        rightward = pltpu.make_async_remote_copy(
            src_ref=to_right,
            dst_ref=right_lands,
            send_sem=halo_send.at[kind, 1],
            recv_sem=halo_recv.at[kind, 1],
            device_id={"space": place + 1},
            device_id_type=MESH,
        )

        def start():
            pl.when(has_left)(leftward.start)
            pl.when(has_right)(rightward.start)

        def arrive():
            pl.when(has_right)(leftward.wait_recv)
            pl.when(has_left)(rightward.wait_recv)

        def sent():
            pl.when(has_left)(leftward.wait_send)
            pl.when(has_right)(rightward.wait_send)

        return start, arrive, sent

    def spread(kind, slabs):
        made = []
        for d, lower, upper in near:
            leftward = pltpu.make_async_remote_copy(
                src_ref=slabs.at[3],
                dst_ref=slabs.at[3 + d],
                send_sem=slab_send.at[kind, 0, d - 1],
                recv_sem=slab_recv.at[kind, 0, d - 1],
                device_id={"space": place - d},
                device_id_type=MESH,
            )
            rightward = pltpu.make_async_remote_copy(
                src_ref=slabs.at[3],
                dst_ref=slabs.at[3 - d],
                send_sem=slab_send.at[kind, 1, d - 1],
                recv_sem=slab_recv.at[kind, 1, d - 1],
                device_id={"space": place + d},
                device_id_type=MESH,
            )
            made.append((lower, upper, leftward, rightward))

        def start():
            for lower, upper, leftward, rightward in made:
                pl.when(lower)(leftward.start)
                pl.when(upper)(rightward.start)

        def arrive():
            for lower, upper, leftward, rightward in made:
                pl.when(upper)(leftward.wait_recv)
                pl.when(lower)(rightward.wait_recv)

        def sent():
            for lower, upper, leftward, rightward in made:
                pl.when(lower)(leftward.wait_send)
                pl.when(upper)(rightward.wait_send)

        return start, arrive, sent

    end = planes + 2
    rhs_copy = exchange(
        0,
        residual.at[0, pl.ds(0, 2)],
        rhs.at[pl.ds(end, 2)],
        residual.at[0, pl.ds(planes - 2, 2)],
        rhs.at[pl.ds(0, 2)],
    )
    cond_copy = exchange(
        1,
        cond.at[pl.ds(3, 3)],
        cond.at[pl.ds(planes + 3, 3)],
        cond.at[pl.ds(planes, 3)],
        cond.at[pl.ds(0, 3)],
    )
    top_copy = exchange(
        2,
        field_b.at[pl.ds(2, 2)],
        top_halo.at[pl.ds(2, 2)],
        field_b.at[pl.ds(planes, 2)],
        top_halo.at[pl.ds(0, 2)],
    )
    cond_mid_copy = exchange(
        3,
        cond_mid.at[pl.ds(2, 2)],
        cond_mid.at[pl.ds(6, 2)],
        cond_mid.at[pl.ds(4, 2)],
        cond_mid.at[pl.ds(0, 2)],
    )
    rhs_mid_copy = exchange(
        4, rhs_mid.at[1], rhs_mid.at[5], rhs_mid.at[4], rhs_mid.at[0]
    )
    mid_copy = exchange(
        5,
        field_mid.at[pl.ds(1, 2)],
        mid_halo.at[pl.ds(2, 2)],
        field_mid.at[pl.ds(3, 2)],
        mid_halo.at[pl.ds(0, 2)],
    )
    cond_low_copy = spread(0, cond_low)
    rhs_low_copy = spread(1, rhs_low)

    rhs_copy[0]()
    for fetch in fetches:
        fetch.wait()

    lattice = (point[...] * generator[...]) & (NPTS - 1)
    shifted = lattice.astype(jnp.float32) / NPTS + offset[...]
    fraction = shifted - jnp.floor(shifted)
    weights = amplitude[...] * (1.0 - 2.0 * jnp.abs(2.0 * fraction - 1.0))

    def conductivity(i):
        along = weights * table_x[pl.ds(place * planes + i, 1), :]
        smooth = exact_dot(table_y[...] * along, table_z[...])
        cond[i + 3] = jnp.exp(log_base[i].astype(jnp.float32) + smooth)

    @pl.loop(0, 3)
    def _(i):
        conductivity(i)
        conductivity(planes - 3 + i)

    cond_copy[0]()

    @pl.loop(0, (planes - 6) // 2)
    def _(i):
        conductivity(3 + 2 * i)
        conductivity(4 + 2 * i)

    half = iota((2 * width, 128), 0)
    lane = iota((2 * width, 128), 1)
    gather_mid = ones_where(lane == 64 * (half // 128) + (half & 127) // 2)
    part = iota((4 * 128, 128), 0)
    lane = iota((4 * 128, 128), 1)
    gather_low = ones_where(lane == 32 * (part // 128) + (part & 63) // 2)

    def to_mid(scale):
        folded = []
        for k in range(4):
            pair = [
                pairs[2 * k + h, pl.ds(0, 64, 2), :] + pairs[2 * k + h, pl.ds(1, 64, 2), :]
                for h in range(2)
            ]
            folded.append(jnp.concatenate(pair, axis=1))
        made = scale * exact_dot(jnp.concatenate(folded, axis=0), gather_mid)
        return made.reshape(4, 64, 128)

    def to_low(scale, source, first):
        folded = [
            source[first + q, pl.ds(0, 32, 2), :] + source[first + q, pl.ds(1, 32, 2), :]
            for q in range(4)
        ]
        return scale * exact_dot(jnp.concatenate(folded, axis=1), gather_low)

    @pl.loop(0, planes // 2)
    def _(i):
        pairs[i] = cond[3 + 2 * i] + cond[4 + 2 * i]

    cond_mid[pl.ds(2, 4)] = to_mid(0.125)
    cond_mid_copy[0]()
    cond_low[3] = to_low(0.125, cond_mid, 2)
    cond_low_copy[0]()

    def block(number):
        inside = jnp.where((number >= 0) & (number < blocks), 1.0, 0.0)
        return mask[(number + blocks) % blocks].astype(jnp.float32) * inside

    cols = mask.shape[1]
    up_top = ones_where(iota((width, cols), 0) // 8 == iota((width, cols), 1))
    out_top = ones_where(iota((cols, 128), 1) // 8 == iota((cols, 128), 0))
    up_mid = ones_where(iota((64, cols), 0) // 4 == iota((64, cols), 1))
    out_mid = ones_where((iota((cols, 128), 1) & 63) // 4 == iota((cols, 128), 0))
    up_low = ones_where(iota((32, cols), 0) // 2 == iota((32, cols), 1))
    col = iota((cols, 128), 1)
    out_low = [
        ones_where(((col & 31) // 2 == iota((cols, 128), 0)) & (col // 64 == h)) for h in range(2)
    ]
    active_mid = []
    for k in range(4):
        one = block(2 * place + k - 1)
        flags[k] = flag_dot(flag_dot(up_top, one), out_top)
        active_mid.append(flag_dot(flag_dot(up_mid, one), out_mid))
    active_mid = jnp.stack([active_mid[j] for j in (0, 1, 1, 2, 2, 3)])
    active_low = []
    for s in range(-3, 4):
        parts = [flag_dot(block(2 * (place + s) + h), out_low[h]) for h in range(2)]
        active_low.append(flag_dot(up_low, parts[0] + parts[1]))
    active_low = jnp.stack(active_low)

    own_rhs.wait()
    edges = sides((width, 128), 128)

    def weigh(i):
        center = cond[i + 1]
        west = 0.5 * (cond[i] + center)
        east = 0.5 * (center + cond[i + 2])
        north, above, total = plane_faces(center, edges)
        total = total + west + east
        face_x[i] = west
        face_x[i + 1] = east
        face_y[i] = north
        face_z[i] = above
        diag[i] = total
        scale = RELAX * flags[(i + 6) // 8] / total
        gain[i] = scale
        field_a[i] = scale * rhs[i]

    def around(source, i):
        total = face_x[i] * source[i - 1] + face_x[i + 1] * source[i + 1]
        return rhs[i] + total + plane_sum(source[i], face_y[i], face_z[i])

    def swept(source, i):
        kept = (1.0 - RELAX) * flags[(i + 6) // 8] * source[i]
        return kept + gain[i] * around(source, i)

    pl.loop(3, planes + 1, unroll=2)(weigh)

    @pl.loop(4, planes, unroll=2)
    def _(i):
        field_b[i] = swept(field_a, i)

    rhs_copy[1]()
    cond_copy[1]()

    @pl.when(place == 0)
    def _():
        for i in range(3):
            cond[i] = cond[3]
        rhs[pl.ds(0, 2)] = jnp.zeros((2, width, 128), jnp.float32)

    @pl.when(place == spaces - 1)
    def _():
        for i in range(3):
            cond[planes + 3 + i] = cond[planes + 2]
        rhs[pl.ds(end, 2)] = jnp.zeros((2, width, 128), jnp.float32)

    @pl.loop(0, 3)
    def _(i):
        weigh(i)
        weigh(planes + 1 + i)

    @pl.loop(0, 3)
    def _(i):
        field_b[1 + i] = swept(field_a, 1 + i)
        field_b[planes + i] = swept(field_a, planes + i)

    top_copy[0]()

    def left_over(i):
        return flags[(i + 6) // 8] * (around(field_b, i) - diag[i] * field_b[i])

    @pl.loop(0, planes // 2)
    def _(i):
        pairs[i] = left_over(2 + 2 * i) + left_over(3 + 2 * i)

    rhs_mid[pl.ds(1, 4)] = to_mid(0.5)
    rhs_mid_copy[0]()

    cond_mid_copy[1]()

    @pl.when(place == 0)
    def _():
        outer = pltpu.roll(cond_mid[2], 64, 1)
        cond_mid[0] = outer
        cond_mid[1] = outer

    @pl.when(place == spaces - 1)
    def _():
        outer = pltpu.roll(cond_mid[5], 64, 1)
        cond_mid[6] = outer
        cond_mid[7] = outer

    east, west, north, above, total = packed_faces(cond_mid[...], 64)
    faces_mid[0] = east
    faces_mid[1] = west
    faces_mid[2] = north
    faces_mid[3] = above
    faces_mid[4] = total
    faces_mid[5] = RELAX * active_mid / total
    faces_mid[6] = active_mid

    rhs_mid_copy[1]()

    @pl.when(place == 0)
    def _():
        rhs_mid[0] = jnp.zeros((64, 128), jnp.float32)

    @pl.when(place == spaces - 1)
    def _():
        rhs_mid[5] = jnp.zeros((64, 128), jnp.float32)

    nothing_mid = jnp.zeros((1, 64, 128), jnp.float32)

    def around_mid(wide):
        return rhs_mid[...] + packed_sum(
            wide, 64, faces_mid[0], faces_mid[1], faces_mid[2], faces_mid[3]
        )

    def swept_mid(wide):
        kept = (1.0 - RELAX) * faces_mid[6] * wide[1:-1]
        return kept + faces_mid[5] * around_mid(wide)

    def widened_mid(value):
        return jnp.concatenate([nothing_mid, value, nothing_mid], axis=0)

    solved_mid = swept_mid(widened_mid(faces_mid[5] * rhs_mid[...]))
    field_mid[...] = solved_mid
    mid_copy[0]()
    rest = faces_mid[6] * (around_mid(widened_mid(solved_mid)) - faces_mid[4] * solved_mid)
    grown_mid[pl.ds(0, 6)] = rest
    rhs_low[3] = to_low(0.5, grown_mid, 1)
    rhs_low_copy[0]()

    cond_low_copy[1]()
    for s in (1, 2, 3):

        @pl.when(place < s)
        def _():
            cond_low[3 - s] = pltpu.roll(cond_low[4 - s], 96, 1)

        @pl.when(place >= spaces - s)
        def _():
            cond_low[3 + s] = pltpu.roll(cond_low[2 + s], 32, 1)

    wide = cond_low[...]
    wide = jnp.concatenate([wide[:1], wide, wide[-1:]], axis=0)
    east, west, north, above, total = packed_faces(wide, 32)
    faces_low[0] = east
    faces_low[1] = west
    faces_low[2] = north
    faces_low[3] = above
    faces_low[4] = RELAX * active_low / total
    faces_low[5] = (1.0 - RELAX) * active_low

    rhs_low_copy[1]()
    for s in (1, 2, 3):

        @pl.when(place < s)
        def _():
            rhs_low[3 - s] = jnp.zeros((32, 128), jnp.float32)

        @pl.when(place >= spaces - s)
        def _():
            rhs_low[3 + s] = jnp.zeros((32, 128), jnp.float32)

    nothing_low = jnp.zeros((1, 32, 128), jnp.float32)
    field_low[...] = faces_low[4] * rhs_low[...]

    @pl.loop(0, SWEEPS_LOW - 1)
    def _(step):
        value = field_low[...]
        wide = jnp.concatenate([nothing_low, value, nothing_low], axis=0)
        total = rhs_low[...] + packed_sum(
            wide, 32, faces_low[0], faces_low[1], faces_low[2], faces_low[3]
        )
        field_low[...] = faces_low[5] * value + faces_low[4] * total

    repeat_low = jnp.where(
        iota((128, 4 * 128), 0)
        == 32 * (iota((128, 4 * 128), 1) // 128) + (iota((128, 4 * 128), 1) & 63) // 2,
        1.0,
        0.0,
    ).astype(jnp.float32)
    grown = exact_dot(field_low[pl.ds(2, 3)].reshape(3 * 32, 128), repeat_low)
    for k in range(-2, 6):
        s, q = (k + 4) // 4, (k + 4) % 4
        piece = grown[32 * s : 32 * s + 32, 128 * q : 128 * q + 128]
        grown_mid[k + 2, pl.ds(0, 32, 2), :] = piece
        grown_mid[k + 2, pl.ds(1, 32, 2), :] = piece

    mid_copy[1]()

    @pl.when(place == 0)
    def _():
        mid_halo[pl.ds(0, 2)] = jnp.zeros((2, 64, 128), jnp.float32)

    @pl.when(place == spaces - 1)
    def _():
        mid_halo[pl.ds(2, 2)] = jnp.zeros((2, 64, 128), jnp.float32)

    wide = grown_mid[...] + jnp.concatenate(
        [mid_halo[pl.ds(0, 2)], field_mid[pl.ds(1, 4)], mid_halo[pl.ds(2, 2)]], axis=0
    )
    solved_mid = swept_mid(widened_mid(swept_mid(wide)))

    repeat_mid = jnp.where(
        iota((128, 256), 0) == 64 * (iota((128, 256), 1) // 128) + (iota((128, 256), 1) & 127) // 2,
        1.0,
        0.0,
    ).astype(jnp.float32)
    grown = exact_dot(solved_mid.reshape(6 * 64, 128), repeat_mid)
    for m in range(-1, planes // 2 + 1):
        k, h = (m + 2) // 2, (m + 2) % 2
        piece = grown[64 * k : 64 * k + 64, 128 * h : 128 * h + 128]
        grown_low[m + 1, pl.ds(0, 64, 2), :] = piece
        grown_low[m + 1, pl.ds(1, 64, 2), :] = piece

    top_copy[1]()

    @pl.when(place == 0)
    def _():
        top_halo[pl.ds(0, 2)] = jnp.zeros((2, width, 128), jnp.float32)

    @pl.when(place == spaces - 1)
    def _():
        top_halo[pl.ds(2, 2)] = jnp.zeros((2, width, 128), jnp.float32)

    for i in range(2):
        field_a[i] = top_halo[i] + grown_low[0]
        field_a[end + i] = top_halo[2 + i] + grown_low[planes // 2 + 1]

    @pl.loop(0, planes // 2)
    def _(i):
        piece = grown_low[i + 1]
        field_a[2 + 2 * i] = field_b[2 + 2 * i] + piece
        field_a[3 + 2 * i] = field_b[3 + 2 * i] + piece

    top_copy[2]()

    chunk = planes // GROUPS
    sends = []
    for g in range(GROUPS):

        @pl.loop(chunk * g + 3 if g else 1, chunk * g + chunk + 3, unroll=2)
        def _(i):
            field_b[i] = swept(field_a, i)

        @pl.loop(0, chunk, unroll=2)
        def _(i):
            correction[0, g * chunk + i] = swept(field_b, g * chunk + i + 2)

        for d in range(1, shifts):
            peer = (shift + d) % shifts
            copy = pltpu.make_async_remote_copy(
                src_ref=correction.at[
                    0, pl.ds(g * chunk, chunk), pl.ds(pl.multiple_of(peer * rows, 8), rows), :
                ],
                dst_ref=arrived.at[d - 1, pl.ds(g * chunk, chunk)],
                send_sem=sum_send.at[d - 1, g],
                recv_sem=sum_recv.at[d - 1, g],
                device_id={"shift": peer},
                device_id_type=MESH,
            )
            copy.start()
            sends.append(copy)

    own_copy = pltpu.make_async_copy(correction, handed, copy_sem.at[10])
    own_copy.start()
    own_rows = pl.ds(pl.multiple_of(shift * rows, 8), rows)
    for g in range(GROUPS):
        span = pl.ds(g * chunk, chunk)
        value = correction[0, span, own_rows, :]
        total, squares = value, value * value
        for d in range(1, shifts):
            sends[g * (shifts - 1) + d - 1].wait_recv()
            value = arrived[d - 1, span]
            total = total + value
            squares = squares + value * value
        mean_field[span] = total / shifts
        square_field[span] = squares / shifts
    for copy in sends:
        copy.wait_send()
    own_copy.wait()
    for group in (rhs_copy, cond_copy, cond_mid_copy, rhs_mid_copy, mid_copy):
        group[2]()
    cond_low_copy[2]()
    rhs_low_copy[2]()


def hand_out(correction, mean_field, square_field, to_correction, to_mean, to_square, sem):
    part = correction.shape[1] // 4
    moves = [
        (correction.at[0, pl.ds(k * part, part)], to_correction.at[0, pl.ds(k * part, part)])
        for k in range(4)
    ]
    moves = moves + [(mean_field, to_mean), (square_field, to_square)]
    copies = [pltpu.make_async_copy(*move, sem.at[n]) for n, move in enumerate(moves)]
    for copy in copies:
        copy.start()
    for copy in copies:
        copy.wait()


def mode_tables(modes):
    order = np.arange(modes)
    along_x = (order % 4 + 1).astype(np.float64)
    along_y = (order // 4 % 4 + 1).astype(np.float64)
    along_z = (order // 16 + 1).astype(np.float64)
    amplitude = 1.5 / np.sqrt(along_x * along_x + along_y * along_y + along_z * along_z)
    return along_x, along_y, along_z, amplitude


def cosines(frequency, cells):
    position = np.arange(cells) + 0.5
    return np.cos(math.pi * frequency[None, :] * position[:, None] / cells).astype(np.float32)


def local(spaces, shifts, residual, log_base, mask, gen_vector, point_index, shift_values):
    planes, width, depth = log_base.shape
    modes = gen_vector.shape[0]
    along_x, along_y, along_z, amplitude = mode_tables(modes)
    table_x = jnp.asarray(cosines(along_x, planes * spaces))
    table_y = jnp.asarray(cosines(along_y, width))
    table_z = jnp.asarray(np.ascontiguousarray(cosines(along_z, depth).T))
    amplitude = jnp.asarray(amplitude.astype(np.float32)[None])
    rows = width // shifts
    f32 = jnp.float32
    vmem = pl.BlockSpec(memory_space=pltpu.VMEM)

    def top(count):
        return pltpu.VMEM((count, width, depth), f32)

    small = (
        log_base,
        mask,
        gen_vector[None],
        point_index[None],
        shift_values,
        table_x,
        table_y,
        table_z,
        amplitude,
    )
    results = pl.pallas_call(
        functools.partial(kernel, spaces, shifts),
        out_shape=(
            jax.ShapeDtypeStruct((1, planes, width, depth), f32),
            jax.ShapeDtypeStruct((planes, rows, depth), f32),
            jax.ShapeDtypeStruct((planes, rows, depth), f32),
        ),
        in_specs=[pl.BlockSpec(memory_space=HBM)] * (1 + len(small)),
        out_specs=(pl.BlockSpec(memory_space=HBM), vmem, vmem),
        scratch_shapes=[
            top(planes + 6),
            top(planes + 4),
            top(planes + 5),
            top(planes + 4),
            top(planes + 4),
            top(planes + 4),
            top(planes + 4),
            top(planes + 4),
            top(planes + 4),
            top(4),
            top(4),
            top(planes // 2),
            pltpu.VMEM((8, 64, 128), f32),
            pltpu.VMEM((6, 64, 128), f32),
            pltpu.VMEM((4, 64, 128), f32),
            pltpu.VMEM((7, 6, 64, 128), f32),
            pltpu.VMEM((6, 64, 128), f32),
            pltpu.VMEM((8, 64, 128), f32),
            pltpu.VMEM((7, 32, 128), f32),
            pltpu.VMEM((7, 32, 128), f32),
            pltpu.VMEM((6, 7, 32, 128), f32),
            pltpu.VMEM((7, 32, 128), f32),
            top(planes // 2 + 2),
            pltpu.VMEM((shifts - 1, planes, rows, depth), f32),
            pltpu.VMEM((1, planes, width, depth), f32),
            *[pltpu.VMEM(array.shape, array.dtype) for array in small],
            pltpu.SemaphoreType.DMA((11,)),
            pltpu.SemaphoreType.DMA((6, 2)),
            pltpu.SemaphoreType.DMA((6, 2)),
            pltpu.SemaphoreType.DMA((2, 2, 3)),
            pltpu.SemaphoreType.DMA((2, 2, 3)),
            pltpu.SemaphoreType.DMA((shifts - 1, GROUPS)),
            pltpu.SemaphoreType.DMA((shifts - 1, GROUPS)),
        ],
        compiler_params=pltpu.CompilerParams(
            collective_id=0, has_side_effects=True, vmem_limit_bytes=63 * 1024 * 1024
        ),
        name="cycle",
    )(
        residual,
        *small,
    )
    hbm = pl.BlockSpec(memory_space=HBM)
    return pl.pallas_call(
        hand_out,
        out_shape=tuple(jax.ShapeDtypeStruct(part.shape, f32) for part in results),
        in_specs=[hbm] * 3,
        out_specs=(hbm,) * 3,
        scratch_shapes=[pltpu.SemaphoreType.DMA((6,))],
        compiler_params=pltpu.CompilerParams(vmem_limit_bytes=63 * 1024 * 1024),
        name="hand_out",
    )(*results)


def solution(mesh):
    placed = (
        P("shift", "space", None, None),
        P("space", None, None),
        P(),
        P(),
        P("shift"),
        P("shift", None),
    )
    return jax.shard_map(
        functools.partial(local, mesh.shape["space"], mesh.shape["shift"]),
        mesh=mesh,
        in_specs=placed,
        out_specs=(
            P("shift", "space", None, None),
            P("space", "shift", None),
            P("space", "shift", None),
        ),
        check_vma=False,
    )
```

```python
import functools
import math

import jax
import jax.numpy as jnp
import numpy as np
from jax import lax
from jax.experimental import pallas as pl
from jax.experimental.pallas import tpu as pltpu
from jax.sharding import PartitionSpec as P

NPTS = 1024
SWEEPS_LOW = 8
RELAX = 0.8
HBM = pltpu.HBM
MESH = pl.DeviceIdType.MESH
HIGHEST = lax.Precision.HIGHEST
GROUPS = 8


def exact_dot(a, b):
    return jnp.dot(a, b, precision=HIGHEST, preferred_element_type=jnp.float32)


def flag_dot(a, b):
    return jnp.dot(
        a.astype(jnp.bfloat16), b.astype(jnp.bfloat16), preferred_element_type=jnp.float32
    )


def iota(shape, dim):
    return lax.broadcasted_iota(jnp.int32, shape, dim)


def ones_where(condition):
    return jnp.where(condition, 1.0, 0.0).astype(jnp.float32)


def ahead(value, axis):
    return pltpu.roll(value, value.shape[axis] - 1, axis)


def behind(value, axis):
    return pltpu.roll(value, 1, axis)


def sides(shape, width):
    nd = len(shape)
    row = iota(shape, nd - 2)
    col = iota(shape, nd - 1) & (width - 1)
    last_row = row == shape[-2] - 1
    last_col = col == width - 1
    extra = ones_where(row == 0) + ones_where(last_row)
    extra = extra + ones_where(col == 0) + ones_where(last_col)
    return last_row, last_col, extra


def plane_faces(center, edges):
    last_row, last_col, extra = edges
    nd = center.ndim
    north = jnp.where(last_row, 0.0, 0.5 * (center + ahead(center, nd - 2)))
    above = jnp.where(last_col, 0.0, 0.5 * (center + ahead(center, nd - 1)))
    total = north + behind(north, nd - 2) + above + behind(above, nd - 1)
    return north, above, total + center * extra


def plane_sum(field, north, above):
    nd = field.ndim
    total = north * ahead(field, nd - 2) + behind(north * field, nd - 2)
    return total + above * ahead(field, nd - 1) + behind(above * field, nd - 1)


def packed_ahead(wide, width):
    upper, lower = wide[1:], wide[:-1]
    lane = iota(upper.shape, 2)
    return pltpu.roll(jnp.where(lane < width, upper, lower), 128 - width, 2)


def packed_behind(wide, width):
    upper, lower = wide[1:], wide[:-1]
    lane = iota(upper.shape, 2)
    return pltpu.roll(jnp.where(lane >= 128 - width, lower, upper), width, 2)


def packed_faces(wide, width):
    center = wide[1:-1]
    east = 0.5 * (center + packed_ahead(wide, width)[1:])
    west = 0.5 * (center + packed_behind(wide, width)[:-1])
    north, above, total = plane_faces(center, sides(center.shape, width))
    return east, west, north, above, total + east + west


def packed_sum(wide, width, east, west, north, above):
    total = east * packed_ahead(wide, width)[1:] + west * packed_behind(wide, width)[:-1]
    return total + plane_sum(wide[1:-1], north, above)


def kernel(
    spaces,
    shifts,
    residual,
    *refs,
):
    sources, refs = refs[:9], refs[9:]
    run(spaces, shifts, residual, sources, *refs)


def run(
    spaces,
    shifts,
    residual,
    sources,
    handed,
    mean_field,
    square_field,
    cond,
    rhs,
    face_x,
    face_y,
    face_z,
    diag,
    gain,
    field_a,
    field_b,
    top_halo,
    flags,
    pairs,
    cond_mid,
    rhs_mid,
    mid_halo,
    faces_mid,
    field_mid,
    grown_mid,
    cond_low,
    rhs_low,
    faces_low,
    field_low,
    grown_low,
    arrived,
    correction,
    log_base,
    mask,
    generator,
    point,
    offset,
    table_x,
    table_y,
    table_z,
    amplitude,
    copy_sem,
    halo_send,
    halo_recv,
    slab_send,
    slab_recv,
    sum_send,
    sum_recv,
):
    shift = lax.axis_index("shift")
    place = lax.axis_index("space")
    planes, width = log_base.shape[0], log_base.shape[1]
    blocks = mask.shape[0]
    has_left = place > 0
    has_right = place < spaces - 1
    rows = width // shifts

    held = (log_base, mask, generator, point, offset, table_x, table_y, table_z, amplitude)
    fetches = [
        pltpu.make_async_copy(source, target, copy_sem.at[n])
        for n, (source, target) in enumerate(zip(sources, held))
    ]
    own_rhs = pltpu.make_async_copy(residual.at[0], rhs.at[pl.ds(2, planes)], copy_sem.at[9])
    for fetch in fetches:
        fetch.start()
    own_rhs.start()
    barrier = pltpu.get_barrier_semaphore()
    near = [(d, place >= d, place < spaces - d) for d in range(1, 4)]
    for d, lower, upper in near:

        @pl.when(lower)
        def _():
            pl.semaphore_signal(barrier, inc=1, device_id={"space": place - d}, device_id_type=MESH)

        @pl.when(upper)
        def _():
            pl.semaphore_signal(barrier, inc=1, device_id={"space": place + d}, device_id_type=MESH)

    for d in range(1, shifts):
        pl.semaphore_signal(
            barrier, inc=1, device_id={"shift": (shift + d) % shifts}, device_id_type=MESH
        )
    peers = shifts - 1
    for d in range(1, 4):
        peers = peers + (place + spaces - d) // spaces + (2 * spaces - 1 - place - d) // spaces
    pl.semaphore_wait(barrier, peers)

    def exchange(kind, to_left, left_lands, to_right, right_lands):
        leftward = pltpu.make_async_remote_copy(
            src_ref=to_left,
            dst_ref=left_lands,
            send_sem=halo_send.at[kind, 0],
            recv_sem=halo_recv.at[kind, 0],
            device_id={"space": place - 1},
            device_id_type=MESH,
        )
        rightward = pltpu.make_async_remote_copy(
            src_ref=to_right,
            dst_ref=right_lands,
            send_sem=halo_send.at[kind, 1],
            recv_sem=halo_recv.at[kind, 1],
            device_id={"space": place + 1},
            device_id_type=MESH,
        )

        def start():
            pl.when(has_left)(leftward.start)
            pl.when(has_right)(rightward.start)

        def arrive():
            pl.when(has_right)(leftward.wait_recv)
            pl.when(has_left)(rightward.wait_recv)

        def sent():
            pl.when(has_left)(leftward.wait_send)
            pl.when(has_right)(rightward.wait_send)

        return start, arrive, sent

    def spread(kind, slabs):
        made = []
        for d, lower, upper in near:
            leftward = pltpu.make_async_remote_copy(
                src_ref=slabs.at[3],
                dst_ref=slabs.at[3 + d],
                send_sem=slab_send.at[kind, 0, d - 1],
                recv_sem=slab_recv.at[kind, 0, d - 1],
                device_id={"space": place - d},
                device_id_type=MESH,
            )
            rightward = pltpu.make_async_remote_copy(
                src_ref=slabs.at[3],
                dst_ref=slabs.at[3 - d],
                send_sem=slab_send.at[kind, 1, d - 1],
                recv_sem=slab_recv.at[kind, 1, d - 1],
                device_id={"space": place + d},
                device_id_type=MESH,
            )
            made.append((lower, upper, leftward, rightward))

        def start():
            for lower, upper, leftward, rightward in made:
                pl.when(lower)(leftward.start)
                pl.when(upper)(rightward.start)

        def arrive():
            for lower, upper, leftward, rightward in made:
                pl.when(upper)(leftward.wait_recv)
                pl.when(lower)(rightward.wait_recv)

        def sent():
            for lower, upper, leftward, rightward in made:
                pl.when(lower)(leftward.wait_send)
                pl.when(upper)(rightward.wait_send)

        return start, arrive, sent

    end = planes + 2
    rhs_copy = exchange(
        0,
        residual.at[0, pl.ds(0, 2)],
        rhs.at[pl.ds(end, 2)],
        residual.at[0, pl.ds(planes - 2, 2)],
        rhs.at[pl.ds(0, 2)],
    )
    cond_copy = exchange(
        1,
        cond.at[pl.ds(3, 3)],
        cond.at[pl.ds(planes + 3, 3)],
        cond.at[pl.ds(planes, 3)],
        cond.at[pl.ds(0, 3)],
    )
    top_copy = exchange(
        2,
        field_b.at[pl.ds(2, 2)],
        top_halo.at[pl.ds(2, 2)],
        field_b.at[pl.ds(planes, 2)],
        top_halo.at[pl.ds(0, 2)],
    )
    cond_mid_copy = exchange(
        3,
        cond_mid.at[pl.ds(2, 2)],
        cond_mid.at[pl.ds(6, 2)],
        cond_mid.at[pl.ds(4, 2)],
        cond_mid.at[pl.ds(0, 2)],
    )
    rhs_mid_copy = exchange(
        4, rhs_mid.at[1], rhs_mid.at[5], rhs_mid.at[4], rhs_mid.at[0]
    )
    mid_copy = exchange(
        5,
        field_mid.at[pl.ds(1, 2)],
        mid_halo.at[pl.ds(2, 2)],
        field_mid.at[pl.ds(3, 2)],
        mid_halo.at[pl.ds(0, 2)],
    )
    cond_low_copy = spread(0, cond_low)
    rhs_low_copy = spread(1, rhs_low)

    rhs_copy[0]()
    for fetch in fetches:
        fetch.wait()

    lattice = (point[...] * generator[...]) & (NPTS - 1)
    shifted = lattice.astype(jnp.float32) / NPTS + offset[...]
    fraction = shifted - jnp.floor(shifted)
    weights = amplitude[...] * (1.0 - 2.0 * jnp.abs(2.0 * fraction - 1.0))

    def conductivity(i):
        along = weights * table_x[pl.ds(place * planes + i, 1), :]
        smooth = exact_dot(table_y[...] * along, table_z[...])
        cond[i + 3] = jnp.exp(log_base[i].astype(jnp.float32) + smooth)

    @pl.loop(0, 3)
    def _(i):
        conductivity(i)
        conductivity(planes - 3 + i)

    cond_copy[0]()

    @pl.loop(0, (planes - 6) // 2)
    def _(i):
        conductivity(3 + 2 * i)
        conductivity(4 + 2 * i)

    half = iota((2 * width, 128), 0)
    lane = iota((2 * width, 128), 1)
    gather_mid = ones_where(lane == 64 * (half // 128) + (half & 127) // 2)
    part = iota((4 * 128, 128), 0)
    lane = iota((4 * 128, 128), 1)
    gather_low = ones_where(lane == 32 * (part // 128) + (part & 63) // 2)

    def to_mid(scale):
        folded = []
        for k in range(4):
            pair = [
                pairs[2 * k + h, pl.ds(0, 64, 2), :] + pairs[2 * k + h, pl.ds(1, 64, 2), :]
                for h in range(2)
            ]
            folded.append(jnp.concatenate(pair, axis=1))
        made = scale * exact_dot(jnp.concatenate(folded, axis=0), gather_mid)
        return made.reshape(4, 64, 128)

    def to_low(scale, source, first):
        folded = [
            source[first + q, pl.ds(0, 32, 2), :] + source[first + q, pl.ds(1, 32, 2), :]
            for q in range(4)
        ]
        return scale * exact_dot(jnp.concatenate(folded, axis=1), gather_low)

    @pl.loop(0, planes // 2)
    def _(i):
        pairs[i] = cond[3 + 2 * i] + cond[4 + 2 * i]

    cond_mid[pl.ds(2, 4)] = to_mid(0.125)
    cond_mid_copy[0]()
    cond_low[3] = to_low(0.125, cond_mid, 2)
    cond_low_copy[0]()

    def block(number):
        inside = jnp.where((number >= 0) & (number < blocks), 1.0, 0.0)
        return mask[(number + blocks) % blocks].astype(jnp.float32) * inside

    cols = mask.shape[1]
    up_top = ones_where(iota((width, cols), 0) // 8 == iota((width, cols), 1))
    out_top = ones_where(iota((cols, 128), 1) // 8 == iota((cols, 128), 0))
    up_mid = ones_where(iota((64, cols), 0) // 4 == iota((64, cols), 1))
    out_mid = ones_where((iota((cols, 128), 1) & 63) // 4 == iota((cols, 128), 0))
    up_low = ones_where(iota((32, cols), 0) // 2 == iota((32, cols), 1))
    col = iota((cols, 128), 1)
    out_low = [
        ones_where(((col & 31) // 2 == iota((cols, 128), 0)) & (col // 64 == h)) for h in range(2)
    ]
    active_mid = []
    for k in range(4):
        one = block(2 * place + k - 1)
        flags[k] = flag_dot(flag_dot(up_top, one), out_top)
        active_mid.append(flag_dot(flag_dot(up_mid, one), out_mid))
    active_mid = jnp.stack([active_mid[j] for j in (0, 1, 1, 2, 2, 3)])
    active_low = []
    for s in range(-3, 4):
        parts = [flag_dot(block(2 * (place + s) + h), out_low[h]) for h in range(2)]
        active_low.append(flag_dot(up_low, parts[0] + parts[1]))
    active_low = jnp.stack(active_low)

    own_rhs.wait()
    edges = sides((width, 128), 128)

    def weigh(i):
        center = cond[i + 1]
        west = 0.5 * (cond[i] + center)
        east = 0.5 * (center + cond[i + 2])
        north, above, total = plane_faces(center, edges)
        total = total + west + east
        face_x[i] = west
        face_x[i + 1] = east
        face_y[i] = north
        face_z[i] = above
        diag[i] = total
        scale = RELAX * flags[(i + 6) // 8] / total
        gain[i] = scale
        field_a[i] = scale * rhs[i]

    def around(source, i):
        total = face_x[i] * source[i - 1] + face_x[i + 1] * source[i + 1]
        return rhs[i] + total + plane_sum(source[i], face_y[i], face_z[i])

    def swept(source, i):
        kept = (1.0 - RELAX) * flags[(i + 6) // 8] * source[i]
        return kept + gain[i] * around(source, i)

    pl.loop(3, planes + 1, unroll=2)(weigh)

    @pl.loop(4, planes, unroll=2)
    def _(i):
        field_b[i] = swept(field_a, i)

    rhs_copy[1]()
    cond_copy[1]()

    @pl.when(place == 0)
    def _():
        for i in range(3):
            cond[i] = cond[3]
        rhs[pl.ds(0, 2)] = jnp.zeros((2, width, 128), jnp.float32)

    @pl.when(place == spaces - 1)
    def _():
        for i in range(3):
            cond[planes + 3 + i] = cond[planes + 2]
        rhs[pl.ds(end, 2)] = jnp.zeros((2, width, 128), jnp.float32)

    @pl.loop(0, 3)
    def _(i):
        weigh(i)
        weigh(planes + 1 + i)

    @pl.loop(0, 3)
    def _(i):
        field_b[1 + i] = swept(field_a, 1 + i)
        field_b[planes + i] = swept(field_a, planes + i)

    top_copy[0]()

    def left_over(i):
        return flags[(i + 6) // 8] * (around(field_b, i) - diag[i] * field_b[i])

    @pl.loop(0, planes // 2)
    def _(i):
        pairs[i] = left_over(2 + 2 * i) + left_over(3 + 2 * i)

    rhs_mid[pl.ds(1, 4)] = to_mid(0.5)
    rhs_mid_copy[0]()

    cond_mid_copy[1]()

    @pl.when(place == 0)
    def _():
        outer = pltpu.roll(cond_mid[2], 64, 1)
        cond_mid[0] = outer
        cond_mid[1] = outer

    @pl.when(place == spaces - 1)
    def _():
        outer = pltpu.roll(cond_mid[5], 64, 1)
        cond_mid[6] = outer
        cond_mid[7] = outer

    east, west, north, above, total = packed_faces(cond_mid[...], 64)
    faces_mid[0] = east
    faces_mid[1] = west
    faces_mid[2] = north
    faces_mid[3] = above
    faces_mid[4] = total
    faces_mid[5] = RELAX * active_mid / total
    faces_mid[6] = active_mid

    rhs_mid_copy[1]()

    @pl.when(place == 0)
    def _():
        rhs_mid[0] = jnp.zeros((64, 128), jnp.float32)

    @pl.when(place == spaces - 1)
    def _():
        rhs_mid[5] = jnp.zeros((64, 128), jnp.float32)

    nothing_mid = jnp.zeros((1, 64, 128), jnp.float32)

    def around_mid(wide):
        return rhs_mid[...] + packed_sum(
            wide, 64, faces_mid[0], faces_mid[1], faces_mid[2], faces_mid[3]
        )

    def swept_mid(wide):
        kept = (1.0 - RELAX) * faces_mid[6] * wide[1:-1]
        return kept + faces_mid[5] * around_mid(wide)

    def widened_mid(value):
        return jnp.concatenate([nothing_mid, value, nothing_mid], axis=0)

    solved_mid = swept_mid(widened_mid(faces_mid[5] * rhs_mid[...]))
    field_mid[...] = solved_mid
    mid_copy[0]()
    rest = faces_mid[6] * (around_mid(widened_mid(solved_mid)) - faces_mid[4] * solved_mid)
    grown_mid[pl.ds(0, 6)] = rest
    rhs_low[3] = to_low(0.5, grown_mid, 1)
    rhs_low_copy[0]()

    cond_low_copy[1]()
    for s in (1, 2, 3):

        @pl.when(place < s)
        def _():
            cond_low[3 - s] = pltpu.roll(cond_low[4 - s], 96, 1)

        @pl.when(place >= spaces - s)
        def _():
            cond_low[3 + s] = pltpu.roll(cond_low[2 + s], 32, 1)

    wide = cond_low[...]
    wide = jnp.concatenate([wide[:1], wide, wide[-1:]], axis=0)
    east, west, north, above, total = packed_faces(wide, 32)
    faces_low[0] = east
    faces_low[1] = west
    faces_low[2] = north
    faces_low[3] = above
    faces_low[4] = RELAX * active_low / total
    faces_low[5] = (1.0 - RELAX) * active_low

    rhs_low_copy[1]()
    for s in (1, 2, 3):

        @pl.when(place < s)
        def _():
            rhs_low[3 - s] = jnp.zeros((32, 128), jnp.float32)

        @pl.when(place >= spaces - s)
        def _():
            rhs_low[3 + s] = jnp.zeros((32, 128), jnp.float32)

    nothing_low = jnp.zeros((1, 32, 128), jnp.float32)
    field_low[...] = faces_low[4] * rhs_low[...]

    @pl.loop(0, SWEEPS_LOW - 1)
    def _(step):
        value = field_low[...]
        wide = jnp.concatenate([nothing_low, value, nothing_low], axis=0)
        total = rhs_low[...] + packed_sum(
            wide, 32, faces_low[0], faces_low[1], faces_low[2], faces_low[3]
        )
        field_low[...] = faces_low[5] * value + faces_low[4] * total

    repeat_low = jnp.where(
        iota((128, 4 * 128), 0)
        == 32 * (iota((128, 4 * 128), 1) // 128) + (iota((128, 4 * 128), 1) & 63) // 2,
        1.0,
        0.0,
    ).astype(jnp.float32)
    grown = exact_dot(field_low[pl.ds(2, 3)].reshape(3 * 32, 128), repeat_low)
    for k in range(-2, 6):
        s, q = (k + 4) // 4, (k + 4) % 4
        piece = grown[32 * s : 32 * s + 32, 128 * q : 128 * q + 128]
        grown_mid[k + 2, pl.ds(0, 32, 2), :] = piece
        grown_mid[k + 2, pl.ds(1, 32, 2), :] = piece

    mid_copy[1]()

    @pl.when(place == 0)
    def _():
        mid_halo[pl.ds(0, 2)] = jnp.zeros((2, 64, 128), jnp.float32)

    @pl.when(place == spaces - 1)
    def _():
        mid_halo[pl.ds(2, 2)] = jnp.zeros((2, 64, 128), jnp.float32)

    wide = grown_mid[...] + jnp.concatenate(
        [mid_halo[pl.ds(0, 2)], field_mid[pl.ds(1, 4)], mid_halo[pl.ds(2, 2)]], axis=0
    )
    solved_mid = swept_mid(widened_mid(swept_mid(wide)))

    repeat_mid = jnp.where(
        iota((128, 256), 0) == 64 * (iota((128, 256), 1) // 128) + (iota((128, 256), 1) & 127) // 2,
        1.0,
        0.0,
    ).astype(jnp.float32)
    grown = exact_dot(solved_mid.reshape(6 * 64, 128), repeat_mid)
    for m in range(-1, planes // 2 + 1):
        k, h = (m + 2) // 2, (m + 2) % 2
        piece = grown[64 * k : 64 * k + 64, 128 * h : 128 * h + 128]
        grown_low[m + 1, pl.ds(0, 64, 2), :] = piece
        grown_low[m + 1, pl.ds(1, 64, 2), :] = piece

    top_copy[1]()

    @pl.when(place == 0)
    def _():
        top_halo[pl.ds(0, 2)] = jnp.zeros((2, width, 128), jnp.float32)

    @pl.when(place == spaces - 1)
    def _():
        top_halo[pl.ds(2, 2)] = jnp.zeros((2, width, 128), jnp.float32)

    for i in range(2):
        field_a[i] = top_halo[i] + grown_low[0]
        field_a[end + i] = top_halo[2 + i] + grown_low[planes // 2 + 1]

    @pl.loop(0, planes // 2)
    def _(i):
        piece = grown_low[i + 1]
        field_a[2 + 2 * i] = field_b[2 + 2 * i] + piece
        field_a[3 + 2 * i] = field_b[3 + 2 * i] + piece

    top_copy[2]()

    chunk = planes // GROUPS
    sends = []
    for g in range(GROUPS):

        @pl.loop(chunk * g + 3 if g else 1, chunk * g + chunk + 3, unroll=2)
        def _(i):
            field_b[i] = swept(field_a, i)

        @pl.loop(0, chunk, unroll=2)
        def _(i):
            correction[0, g * chunk + i] = swept(field_b, g * chunk + i + 2)

        for d in range(1, shifts):
            peer = (shift + d) % shifts
            copy = pltpu.make_async_remote_copy(
                src_ref=correction.at[
                    0, pl.ds(g * chunk, chunk), pl.ds(pl.multiple_of(peer * rows, 8), rows), :
                ],
                dst_ref=arrived.at[d - 1, pl.ds(g * chunk, chunk)],
                send_sem=sum_send.at[d - 1, g],
                recv_sem=sum_recv.at[d - 1, g],
                device_id={"shift": peer},
                device_id_type=MESH,
            )
            copy.start()
            sends.append(copy)

    own_copy = pltpu.make_async_copy(correction, handed, copy_sem.at[10])
    own_copy.start()
    own_rows = pl.ds(pl.multiple_of(shift * rows, 8), rows)
    for g in range(GROUPS):
        span = pl.ds(g * chunk, chunk)
        value = correction[0, span, own_rows, :]
        total, squares = value, value * value
        for d in range(1, shifts):
            sends[g * (shifts - 1) + d - 1].wait_recv()
            value = arrived[d - 1, span]
            total = total + value
            squares = squares + value * value
        mean_field[span] = total / shifts
        square_field[span] = squares / shifts
    for copy in sends:
        copy.wait_send()
    own_copy.wait()
    for group in (rhs_copy, cond_copy, cond_mid_copy, rhs_mid_copy, mid_copy):
        group[2]()
    cond_low_copy[2]()
    rhs_low_copy[2]()


def hand_out(
    correction, mean_field, square_field, to_correction, to_mean, to_square, *held_and_sems
):
    held_correction, held_mean, held_square, in_sem, out_sem = held_and_sems
    part = correction.shape[1] // 4
    moves = []
    for k in range(4):
        span = pl.ds(k * part, part)
        moves.append(
            (correction.at[0, span], held_correction.at[0, span], to_correction.at[0, span])
        )
    moves.append((mean_field, held_mean, to_mean))
    moves.append((square_field, held_square, to_square))
    fetches = [pltpu.make_async_copy(m[0], m[1], in_sem.at[n]) for n, m in enumerate(moves)]
    stores = [pltpu.make_async_copy(m[1], m[2], out_sem.at[n]) for n, m in enumerate(moves)]
    for fetch in fetches:
        fetch.start()
    for fetch, store in zip(fetches, stores):
        fetch.wait()
        store.start()
    for store in stores:
        store.wait()


def mode_tables(modes):
    order = np.arange(modes)
    along_x = (order % 4 + 1).astype(np.float64)
    along_y = (order // 4 % 4 + 1).astype(np.float64)
    along_z = (order // 16 + 1).astype(np.float64)
    amplitude = 1.5 / np.sqrt(along_x * along_x + along_y * along_y + along_z * along_z)
    return along_x, along_y, along_z, amplitude


def cosines(frequency, cells):
    position = np.arange(cells) + 0.5
    return np.cos(math.pi * frequency[None, :] * position[:, None] / cells).astype(np.float32)


def local(spaces, shifts, residual, log_base, mask, gen_vector, point_index, shift_values):
    planes, width, depth = log_base.shape
    modes = gen_vector.shape[0]
    along_x, along_y, along_z, amplitude = mode_tables(modes)
    table_x = jnp.asarray(cosines(along_x, planes * spaces))
    table_y = jnp.asarray(cosines(along_y, width))
    table_z = jnp.asarray(np.ascontiguousarray(cosines(along_z, depth).T))
    amplitude = jnp.asarray(amplitude.astype(np.float32)[None])
    rows = width // shifts
    f32 = jnp.float32
    vmem = pl.BlockSpec(memory_space=pltpu.VMEM)

    def top(count):
        return pltpu.VMEM((count, width, depth), f32)

    small = (
        log_base,
        mask,
        gen_vector[None],
        point_index[None],
        shift_values,
        table_x,
        table_y,
        table_z,
        amplitude,
    )
    results = pl.pallas_call(
        functools.partial(kernel, spaces, shifts),
        out_shape=(
            jax.ShapeDtypeStruct((1, planes, width, depth), f32),
            jax.ShapeDtypeStruct((planes, rows, depth), f32),
            jax.ShapeDtypeStruct((planes, rows, depth), f32),
        ),
        in_specs=[pl.BlockSpec(memory_space=HBM)] * (1 + len(small)),
        out_specs=(pl.BlockSpec(memory_space=HBM), vmem, vmem),
        scratch_shapes=[
            top(planes + 6),
            top(planes + 4),
            top(planes + 5),
            top(planes + 4),
            top(planes + 4),
            top(planes + 4),
            top(planes + 4),
            top(planes + 4),
            top(planes + 4),
            top(4),
            top(4),
            top(planes // 2),
            pltpu.VMEM((8, 64, 128), f32),
            pltpu.VMEM((6, 64, 128), f32),
            pltpu.VMEM((4, 64, 128), f32),
            pltpu.VMEM((7, 6, 64, 128), f32),
            pltpu.VMEM((6, 64, 128), f32),
            pltpu.VMEM((8, 64, 128), f32),
            pltpu.VMEM((7, 32, 128), f32),
            pltpu.VMEM((7, 32, 128), f32),
            pltpu.VMEM((6, 7, 32, 128), f32),
            pltpu.VMEM((7, 32, 128), f32),
            top(planes // 2 + 2),
            pltpu.VMEM((shifts - 1, planes, rows, depth), f32),
            pltpu.VMEM((1, planes, width, depth), f32),
            *[pltpu.VMEM(array.shape, array.dtype) for array in small],
            pltpu.SemaphoreType.DMA((11,)),
            pltpu.SemaphoreType.DMA((6, 2)),
            pltpu.SemaphoreType.DMA((6, 2)),
            pltpu.SemaphoreType.DMA((2, 2, 3)),
            pltpu.SemaphoreType.DMA((2, 2, 3)),
            pltpu.SemaphoreType.DMA((shifts - 1, GROUPS)),
            pltpu.SemaphoreType.DMA((shifts - 1, GROUPS)),
        ],
        compiler_params=pltpu.CompilerParams(
            collective_id=0, has_side_effects=True, vmem_limit_bytes=63 * 1024 * 1024
        ),
        name="cycle",
    )(
        residual,
        *small,
    )
    hbm = pl.BlockSpec(memory_space=HBM)
    return pl.pallas_call(
        hand_out,
        out_shape=tuple(jax.ShapeDtypeStruct(part.shape, f32) for part in results),
        in_specs=[hbm] * 3,
        out_specs=(hbm,) * 3,
        scratch_shapes=[
            *[pltpu.VMEM(part.shape, f32) for part in results],
            pltpu.SemaphoreType.DMA((6,)),
            pltpu.SemaphoreType.DMA((6,)),
        ],
        compiler_params=pltpu.CompilerParams(vmem_limit_bytes=63 * 1024 * 1024),
        name="hand_out",
    )(*results)


def solution(mesh):
    placed = (
        P("shift", "space", None, None),
        P("space", None, None),
        P(),
        P(),
        P("shift"),
        P("shift", None),
    )
    return jax.shard_map(
        functools.partial(local, mesh.shape["space"], mesh.shape["shift"]),
        mesh=mesh,
        in_specs=placed,
        out_specs=(
            P("shift", "space", None, None),
            P("space", "shift", None),
            P("space", "shift", None),
        ),
        check_vma=False,
    )
```
